128 devices in a mesh: dom: 16 (over z, y_lo, core), band: 8 (over x, y_hi).
Axes of the slice: x: 4, y: 4 (y_hi: 2, y_lo: 2; y = y_hi * 2 + y_lo), z: 4, core: 2. Of those that a mesh axis runs over, the one named last changes fastest.
Arguments:
- wavefunctions: bfloat16 [39168, 1024], P('dom', 'band')
- cell_hamiltonian: bfloat16 [512, 125, 125], P('dom')
- cell_nodes: int32 [512, 125], P('dom'), may hold values from 0 to 2600, as said below
- face_nodes: int32 [2448], P('dom'), may hold values from 0 to 2447, as said below
Outputs:
- filtered: bfloat16 [39168, 1024], P('dom', 'band')
- correlation: float32 [1024, 1024], P('dom', 'band')
- projected: float32 [1024, 1024], P('dom', 'band')
The draws below stay inside these ranges and needn't reach their ends.
Inputs may be any that keep to these rules, and one draw needn't show every extreme that they name: `cell_nodes`: cells come in 16 runs of 32, one run a domain. Cell r of a run sits at x = r mod 2, y = (r div 2) mod 4, z = r div (8) of the domain's grid of cells, and its slot a = i + 5 j + 25 k names grid node (4 x + i, 4 y + j, 4 z + k) of the domain's grid of nodes. Grid nodes whose third coordinate is below 16 are the domain's own nodes, one local number each, all distinct. Node (p, q, 16) is named 2448 + q * 9 + p. `face_nodes`: entry f of a domain's 153 entries is the local number of its grid node (f mod (9), f div (9), 0) in the grid of cell_nodes.
All inputs are finite; a program needn't handle non-finite values.
Results may differ from the reference program's by a relative error of at most 0.013.
Values may be sent and summed in bfloat16 or wider, within the bound.
A program may use at most 64 MiB of HBM per device.

```python
import jax
import jax.numpy as jnp
from jax import lax

CX = 2
CY = 4
CZ = 4
CELL_DEV = 32
FACE = 153
NODE_DEV = 2448
NODES = 39168
CELLS = 512
WAVES = 1024
N_DOM = 16


def place_value(order, value, position):
    where = jnp.argmax(order == value).astype(jnp.int32)
    displaced = order[position]
    return order.at[where].set(displaced).at[position].set(value)


def local_order(key):
    keys = jax.random.split(key, NODES // NODE_DEV)

    def single_order(single):
        order = jax.random.permutation(single, NODE_DEV).astype(jnp.int32)
        order = place_value(order, NODE_DEV - 1, 0)
        return place_value(order, 0, 1)
    return jax.vmap(single_order)(keys)


def draw_cell_nodes(key, part):
    order = local_order(key)
    row_len = 4 * CX + 1
    col_len = 4 * CY + 1
    cell_ids = jnp.arange(CELL_DEV, dtype=jnp.int32)
    node_ids = jnp.arange(125, dtype=jnp.int32)
    xpos = 4 * (cell_ids % CX)[:, None] + (node_ids % 5)[None, :]
    ypos = 4 * (cell_ids // CX % CY)[:, None] + (node_ids // 5 % 5)[None, :]
    zpos = 4 * (cell_ids // (CX * CY))[:, None] + (node_ids // 25)[None, :]
    canon = (zpos * col_len + ypos) * row_len + xpos
    canon = jnp.minimum(canon, NODE_DEV - 1)
    borrowed = NODE_DEV + ypos * row_len + xpos
    local = jnp.take(order, canon.reshape(-1), axis=1).reshape(-1, CELL_DEV, 125)
    chosen = jnp.where((zpos == 4 * CZ)[None, :, :], borrowed[None, :, :], local)
    return chosen.reshape(CELLS, 125).astype(jnp.int32)


def draw_face_nodes(key, part):
    order = local_order(key)
    return order[:, :FACE].reshape(-1).astype(jnp.int32)


def draw_cell_hamiltonian(key, part):
    key = jax.random.fold_in(key, 5)
    first_key, second_key = jax.random.split(key)
    raw = jax.random.normal(first_key, (CELLS, 125, 125), jnp.float32)
    shift = jax.random.uniform(second_key, (CELLS, 125), jnp.float32, 0.0, 0.1)
    symmetric = (raw + jnp.swapaxes(raw, 1, 2)) * (0.7071 / 31.6)
    diagonal = jnp.eye(125, dtype=jnp.float32)[None, :, :] * shift[:, :, None]
    return (symmetric + diagonal).astype(jnp.bfloat16)


def draw_wavefunctions(key, part):
    key = jax.random.fold_in(key, 7)
    first_key, second_key, third_key = jax.random.split(key, 3)
    common = jax.random.normal(second_key, (NODES, 1), jnp.float32)
    across = jax.random.normal(third_key, (1, WAVES), jnp.float32)
    noise = jax.random.normal(first_key, (NODES, WAVES), jnp.float32)
    values = noise + 0.7 * common * across
    return jnp.clip(values, -8.0, 8.0).astype(jnp.bfloat16)


def setup_inputs(seed: int = 0) -> dict:
    streams_of = jax.random.split(jax.random.key(seed), 5)
    return {
        "wavefunctions": draw_wavefunctions(jax.random.fold_in(streams_of[4], 71), 0),
        "cell_hamiltonian": draw_cell_hamiltonian(jax.random.fold_in(streams_of[4], 71), 0),
        "cell_nodes": draw_cell_nodes(jax.random.fold_in(streams_of[4], 71), 0),
        "face_nodes": draw_face_nodes(jax.random.fold_in(streams_of[4], 71), 0),
    }


filter_center = 1.0
filter_half = 1.5


def apply_operator(values, cell_hamiltonian, cell_nodes, face_nodes):
    def domain_terms(domain):
        later = (domain + 1) % N_DOM
        owned = lax.dynamic_slice_in_dim(values, (domain * NODE_DEV).astype(jnp.int32), NODE_DEV, 0)
        neighbour = lax.dynamic_slice_in_dim(values, (later * NODE_DEV).astype(jnp.int32), NODE_DEV, 0)
        later_faces = lax.dynamic_slice_in_dim(face_nodes, (later * FACE).astype(jnp.int32), FACE, 0)
        ghosts = jnp.take(neighbour, later_faces, axis=0)
        extended = jnp.concatenate([owned, ghosts], axis=0)
        nodes_here = lax.dynamic_slice_in_dim(cell_nodes, (domain * CELL_DEV).astype(jnp.int32), CELL_DEV, 0)
        blocks = lax.dynamic_slice_in_dim(cell_hamiltonian, (domain * CELL_DEV).astype(jnp.int32), CELL_DEV, 0)
        gathered = jnp.take(extended, nodes_here, axis=0)
        product = jnp.einsum("cij,cjw->ciw", blocks.astype(jnp.float32), gathered.astype(jnp.float32))
        summed = jax.ops.segment_sum(product.reshape(-1, values.shape[1]), nodes_here.reshape(-1), num_segments=NODE_DEV + FACE)
        return summed[:NODE_DEV], summed[NODE_DEV:]

    owned_sums, outgoing = lax.map(domain_terms, jnp.arange(N_DOM, dtype=jnp.int32))
    incoming = jnp.roll(outgoing, 1, axis=0)
    faces = face_nodes.reshape(N_DOM, FACE)
    merged = jax.vmap(lambda rows, where, extra: rows.at[where].add(extra))(owned_sums, faces, incoming)
    return merged.reshape(NODES, values.shape[1])


def reference(wavefunctions, cell_hamiltonian, cell_nodes, face_nodes):
    start = wavefunctions.astype(jnp.float32)
    first = apply_operator(wavefunctions, cell_hamiltonian, cell_nodes, face_nodes)
    section_one = ((first - filter_center * start) / filter_half).astype(jnp.bfloat16)
    second = apply_operator(section_one, cell_hamiltonian, cell_nodes, face_nodes)
    filtered = (2.0 * (second - filter_center * section_one.astype(jnp.float32)) / filter_half - start).astype(jnp.bfloat16)
    image = apply_operator(filtered, cell_hamiltonian, cell_nodes, face_nodes).astype(jnp.bfloat16)
    correlation = jnp.dot(filtered.T, filtered, preferred_element_type=jnp.float32) / NODES
    projected = jnp.dot(filtered.T, image, preferred_element_type=jnp.float32) / NODES
    return filtered, correlation, projected
```

```python
import jax
import jax.numpy as jnp
import numpy as np
from jax import lax
from jax.experimental import pallas as pl
from jax.experimental.pallas import tpu as pltpu
from jax.sharding import PartitionSpec as P

CX, CY, CZ = 2, 4, 4
LINE = 4 * CX + 1
COL = 4 * CY + 1
PLANE = LINE * COL
OWN = 4 * CZ * PLANE
FACE_PAD = 160
GRID = OWN + FACE_PAD
RUN = 5 * LINE
RUN_PAD = 48
PAIR = 5 * RUN_PAD
PAIRS = CY * CZ
LAYER = 4 * PLANE
SLAB = 768
NX = 4
WAVE = 128
SORTED = 2560

filter_center = 1.0
filter_half = 1.5

f32 = jnp.float32
bf16 = jnp.bfloat16
MESH = pl.DeviceIdType.MESH


def expansion():
    e = np.zeros((PAIR, 2 * 128), np.float32)
    for k in range(5):
        for j in range(5):
            for x in range(LINE):
                for cell in range(CX):
                    i = x - 4 * cell
                    if 0 <= i < 5:
                        e[RUN_PAD * k + LINE * j + x, 128 * cell + i + 5 * j + 25 * k] = 1
    return e


def kernel(
    w_ref,
    h_ref,
    nodes_ref,
    e_ref,
    et_ref,
    filtered_ref,
    corr_ref,
    proj_ref,
    w32,
    ident,
    order,
    start,
    section,
    total,
    pairs,
    face_out,
    face_in,
    back_out,
    back_in,
    slabs,
    waves,
    compact,
    restored,
    piece,
    image,
    right,
    gram,
    from_core,
    half,
    from_x,
    quarter,
    final,
    face_s,
    face_r,
    back_s,
    back_r,
    x_s,
    x_r,
    y_s,
    y_r,
    core_s,
    core_r,
    red_s,
    red_r,
    fin_s,
    fin_r,
    out_s,
):
    d = lax.axis_index("dom")
    b = lax.axis_index("band")
    n_dom = lax.axis_size("dom")
    chip = lax.div(d, 2)
    core = lax.rem(d, 2)
    x = lax.div(b, 2)
    yh = lax.rem(b, 2)
    yl = lax.rem(chip, 2)
    prev = lax.rem(d + n_dom - 1, n_dom)
    succ = lax.rem(d + 1, n_dom)
    mate = (2 * chip + 1 - core, b)
    across = (d, 2 * x + 1 - yh)

    def along_x(xx):
        return (d, 2 * xx + yh)

    def other_chip(cc):
        return (2 * cc + core, b)

    barrier = pltpu.get_barrier_semaphore()
    greeted = [(prev, b), (succ, b), mate, across]
    greeted += [along_x(lax.rem(x + off, NX)) for off in range(1, NX)]
    greeted += [other_chip(lax.rem(chip + off, 8)) for off in range(1, 8)]
    for device in greeted:
        pl.semaphore_signal(barrier, inc=1, device_id=device, device_id_type=MESH)

    w32[...] = w_ref[...].astype(f32)

    def gather_plane(zz, carry):
        cz = lax.div(zz, 4)
        k = zz - 4 * cz
        for q in range(COL):
            cy = min(q // 4, CY - 1)
            for p in range(LINE):
                cx = min(p // 4, CX - 1)
                slot = (p - 4 * cx) + 5 * (q - 4 * cy)
                node = nodes_ref[cz * (CX * CY) + cy * CX + cx, slot + 25 * k]
                row = zz * PLANE + q * LINE + p
                start[pl.ds(row, 1), :] = w32[pl.ds(node, 1), :]
                ident[pl.ds(row, 1), :] = jnp.full((1, WAVE), node, jnp.int32)
        return carry

    lax.fori_loop(0, 4 * CZ, gather_plane, 0)
    pl.semaphore_wait(barrier, len(greeted))

    def face_copy(n):
        return pltpu.make_async_remote_copy(
            src_ref=face_out.at[n],
            dst_ref=face_in.at[n],
            send_sem=face_s.at[n],
            recv_sem=face_r.at[n],
            device_id=(prev, b),
            device_id_type=MESH,
        )

    def back_copy(n):
        return pltpu.make_async_remote_copy(
            src_ref=back_out.at[n],
            dst_ref=back_in.at[n],
            send_sem=back_s.at[n],
            recv_sem=back_r.at[n],
            device_id=(succ, b),
            device_id_type=MESH,
        )

    def send_face(n, field):
        face_out[n] = field[0:FACE_PAD, :].astype(bf16)
        face_copy(n).start()

    def take_face(n, field):
        face_copy(n).wait_recv()
        field[OWN:GRID, :] = face_in[n].astype(f32)

    def add_pair(block, base, source, target):
        rows = [source[base + PLANE * k : base + PLANE * k + RUN_PAD, :] for k in range(5)]
        rows = [r.astype(bf16) for r in rows] + [jnp.zeros((16, WAVE), bf16)]
        result = jnp.dot(block, jnp.concatenate(rows, axis=0), preferred_element_type=f32)
        for k in range(5):
            at = base + PLANE * k
            target[at : at + RUN_PAD, :] += result[RUN_PAD * k : RUN_PAD * (k + 1)]

    def clear(ref):
        def tile(i, carry):
            ref[pl.ds(pl.multiple_of(16 * i, 16), 16), :] = jnp.zeros((16, WAVE), f32)
            return carry

        lax.fori_loop(0, ref.shape[0] // 16, tile, 0)

    def add_layer(cz, source):
        for cy in range(CY):
            add_pair(pairs[CY * cz + cy], LAYER * cz + 4 * LINE * cy, source, total)

    send_face(0, start)

    for p in range(PAIRS):
        block = None
        for cell in range(CX):
            at = 128 * cell
            rows = jnp.dot(
                e_ref[:, at : at + 125], h_ref[CX * p + cell], preferred_element_type=f32
            ).astype(bf16)
            part = jnp.dot(rows, et_ref[at : at + 125, :], preferred_element_type=f32)
            block = part if block is None else block + part
        pairs[p] = block.astype(bf16)

    def first_half(n, source):
        clear(total)
        add_layer(0, source)
        add_layer(1, source)
        take_face(n, source)
        add_layer(3, source)
        back_out[n] = total[OWN:GRID, :]
        back_copy(n).start()
        add_layer(2, source)

    def take_back(n):
        back_copy(n).wait_recv()
        total[0:FACE_PAD, :] += back_in[n]

    def to_section(lo, hi):
        value = (total[lo:hi, :] - filter_center * start[lo:hi, :]) * (1.0 / filter_half)
        section[lo:hi, :] = value.astype(bf16).astype(f32)

    def to_filtered(lo, hi):
        value = (total[lo:hi, :] - filter_center * section[lo:hi, :]) * (2.0 / filter_half)
        value = (value - start[lo:hi, :]).astype(bf16)
        compact[lo:hi, :] = value
        start[lo:hi, :] = value.astype(f32)

    first_half(0, start)
    to_section(FACE_PAD, OWN)
    take_back(0)
    to_section(0, FACE_PAD)
    send_face(1, section)
    first_half(1, section)
    to_filtered(FACE_PAD, OWN)

    def x_copy(j):
        return pltpu.make_async_remote_copy(
            src_ref=slabs.at[j],
            dst_ref=waves.at[x],
            send_sem=x_s.at[j],
            recv_sem=x_r.at[x],
            device_id=along_x(j),
            device_id_type=MESH,
        )

    def x_arrival(xx):
        return pltpu.make_async_remote_copy(
            src_ref=slabs.at[0],
            dst_ref=waves.at[xx],
            send_sem=x_s.at[0],
            recv_sem=x_r.at[xx],
            device_id=along_x(xx),
            device_id_type=MESH,
        )

    def y_copy(xx):
        return pltpu.make_async_remote_copy(
            src_ref=waves.at[xx],
            dst_ref=waves.at[NX + xx],
            send_sem=y_s.at[xx],
            recv_sem=y_r.at[xx],
            device_id=across,
            device_id_type=MESH,
        )

    def send_slab(j):
        slabs[j] = start[LAYER * j : LAYER * j + SLAB, :].astype(bf16)

        @pl.when(x != j)
        def _():
            x_copy(j).start()

        @pl.when(x == j)
        def _():
            waves[j] = slabs[j]
            y_copy(j).start()

    send_slab(1)
    send_slab(2)
    take_back(1)
    to_filtered(0, FACE_PAD)
    send_face(2, start)
    send_slab(0)
    take_face(2, start)
    send_slab(3)

    compact[OWN:SORTED, :] = jnp.zeros((SORTED - OWN, WAVE), bf16)
    ident[OWN:SORTED, :] = jnp.full((SORTED - OWN, WAVE), -1, jnp.int32)
    for t in range(SORTED // WAVE):
        order[:, WAVE * t : WAVE * (t + 1)] = ident[WAVE * t : WAVE * (t + 1), :].T[:8]

    def restore(lo, hi):
        rows = lax.broadcasted_iota(jnp.int32, (hi - lo, 256), 0) + lo
        value = jnp.zeros((hi - lo, WAVE), f32)
        for t in range(SORTED // 256):
            here = jnp.broadcast_to(order[0:1, 256 * t : 256 * (t + 1)], (hi - lo, 256))
            hit = jnp.where(rows == here, 1.0, 0.0).astype(bf16)
            value += jnp.dot(hit, compact[256 * t : 256 * (t + 1), :], preferred_element_type=f32)
        restored[lo:hi, :] = value.astype(bf16)

    def out_copy():
        return pltpu.make_async_copy(restored, filtered_ref, out_s)

    own_rows = lax.broadcasted_iota(jnp.int32, (SLAB, WAVE), 0) < LAYER

    def take_piece(xx):
        piece[...] = waves[xx].astype(f32)
        clear(image)
        for cy in range(CY):
            add_pair(pairs[CY * x + cy], 4 * LINE * cy, piece, image)
        at = pl.multiple_of(2 * WAVE * xx, 2 * WAVE)
        right[:, pl.ds(at, WAVE)] = jnp.where(own_rows, piece[...], 0.0).astype(bf16)
        right[:, pl.ds(at + WAVE, WAVE)] = image[...].astype(bf16)

    take_piece(x)
    restore(0, 640)
    for off, lo, hi in ((1, 640, 1280), (3, 1280, 1920), (2, 1920, OWN)):
        xx = lax.rem(x + off, NX)
        x_arrival(xx).wait_recv()
        y_copy(xx).start()
        take_piece(xx)
        restore(lo, hi)
    out_copy().start()

    keep = pl.multiple_of(64 * core, 64)
    give = pl.multiple_of(64 * (1 - core), 64)

    def core_copy(t):
        return pltpu.make_async_remote_copy(
            src_ref=gram.at[t, pl.ds(give, 64)],
            dst_ref=from_core.at[t],
            send_sem=core_s.at[t],
            recv_sem=core_r.at[t],
            device_id=mate,
            device_id_type=MESH,
        )

    def block_of(xx):
        return pl.ds(pl.multiple_of(2 * WAVE * xx, 2 * WAVE), 2 * WAVE)

    def red_copy(t, xx):
        return pltpu.make_async_remote_copy(
            src_ref=half.at[t, :, block_of(xx)],
            dst_ref=from_x.at[t, x],
            send_sem=red_s.at[t, xx],
            recv_sem=red_r.at[t, x],
            device_id=along_x(xx),
            device_id_type=MESH,
        )

    def red_arrival(t, xx):
        return pltpu.make_async_remote_copy(
            src_ref=half.at[t, :, block_of(xx)],
            dst_ref=from_x.at[t, xx],
            send_sem=red_s.at[t, xx],
            recv_sem=red_r.at[t, xx],
            device_id=along_x(xx),
            device_id_type=MESH,
        )

    def target_chip(t):
        band_side = jnp.where(t < NX, yh, 1 - yh)
        return 2 * lax.rem(t, NX) + band_side

    def fin_copy(t):
        return pltpu.make_async_remote_copy(
            src_ref=quarter.at[t],
            dst_ref=final.at[chip],
            send_sem=fin_s.at[t],
            recv_sem=fin_r.at[chip],
            device_id=other_chip(target_chip(t)),
            device_id_type=MESH,
        )

    def fin_arrival(cc):
        return pltpu.make_async_remote_copy(
            src_ref=quarter.at[0],
            dst_ref=final.at[cc],
            send_sem=fin_s.at[0],
            recv_sem=fin_r.at[cc],
            device_id=other_chip(cc),
            device_id_type=MESH,
        )

    def multiply(t):
        gram[t] = lax.dot_general(
            waves[t], right[...], (((0,), (0,)), ((), ())), preferred_element_type=f32
        ).astype(bf16)
        core_copy(t).start()

    def sum_core(t):
        core_copy(t).wait_recv()
        value = gram[t, pl.ds(keep, 64), :].astype(f32) + from_core[t].astype(f32)
        half[t] = value.astype(bf16)
        for off in range(1, NX):
            red_copy(t, lax.rem(x + off, NX)).start()

    def sum_x(t):
        value = half[t, :, block_of(x)].astype(f32)
        for off in range(1, NX):
            xx = lax.rem(x + off, NX)
            red_arrival(t, xx).wait_recv()
            value += from_x[t, xx].astype(f32)
        quarter[t] = value.astype(bf16)
        away = target_chip(t) != chip

        @pl.when(away)
        def _():
            fin_copy(t).start()

        @pl.when(jnp.logical_not(away))
        def _():
            final[chip] = quarter[t]

    def band_round(t, carry):
        @pl.when(jnp.logical_and(t >= NX, t < 2 * NX))
        def _():
            y_copy(t - NX).wait_recv()

        @pl.when(t < 2 * NX)
        def _():
            multiply(t)

        @pl.when(jnp.logical_and(t >= 1, t < 2 * NX + 1))
        def _():
            sum_core(t - 1)

        @pl.when(t >= 2)
        def _():
            sum_x(t - 2)

        return carry

    lax.fori_loop(0, 2 * NX + 2, band_round, 0)

    for cc in range(8):

        @pl.when(chip != cc)
        def _():
            fin_arrival(cc).wait_recv()

    result = final[0].astype(f32)
    for cc in range(1, 8):
        result += final[cc].astype(f32)
    result = result * (1.0 / (n_dom * OWN))
    corr_ref[...] = result[:, :WAVE]
    proj_ref[...] = result[:, WAVE:]

    for n in range(3):
        face_copy(n).wait_send()
    for n in range(2):
        back_copy(n).wait_send()
    for j in range(NX):

        @pl.when(x != j)
        def _():
            x_copy(j).wait_send()

        y_copy(j).wait_send()

    def drain(t, carry):
        core_copy(t).wait_send()
        for off in range(1, NX):
            red_copy(t, lax.rem(x + off, NX)).wait_send()

        @pl.when(target_chip(t) != chip)
        def _():
            fin_copy(t).wait_send()

        return carry

    lax.fori_loop(0, 2 * NX, drain, 0)
    out_copy().wait()


def shards(wavefunctions, cell_hamiltonian, cell_nodes, face_nodes):
    e = expansion()
    expand = jnp.asarray(e, bf16)
    expand_t = jnp.asarray(np.pad(e.T, ((0, 0), (0, 256 - PAIR))), bf16)
    vmem = pl.BlockSpec(memory_space=pltpu.VMEM)
    dma = pltpu.SemaphoreType.DMA
    return pl.pallas_call(
        kernel,
        out_shape=(
            jax.ShapeDtypeStruct((OWN, WAVE), bf16),
            jax.ShapeDtypeStruct((64, WAVE), f32),
            jax.ShapeDtypeStruct((64, WAVE), f32),
        ),
        in_specs=[vmem, vmem, pl.BlockSpec(memory_space=pltpu.SMEM), vmem, vmem],
        out_specs=(pl.BlockSpec(memory_space=pl.ANY), vmem, vmem),
        scratch_shapes=[
            pltpu.VMEM((OWN, WAVE), f32),
            pltpu.VMEM((SORTED, WAVE), jnp.int32),
            pltpu.VMEM((8, SORTED), jnp.int32),
            pltpu.VMEM((GRID, WAVE), f32),
            pltpu.VMEM((GRID, WAVE), f32),
            pltpu.VMEM((GRID, WAVE), f32),
            pltpu.VMEM((PAIRS, PAIR, 256), bf16),
            pltpu.VMEM((3, FACE_PAD, WAVE), bf16),
            pltpu.VMEM((3, FACE_PAD, WAVE), bf16),
            pltpu.VMEM((2, FACE_PAD, WAVE), f32),
            pltpu.VMEM((2, FACE_PAD, WAVE), f32),
            pltpu.VMEM((NX, SLAB, WAVE), bf16),
            pltpu.VMEM((2 * NX, SLAB, WAVE), bf16),
            pltpu.VMEM((SORTED, WAVE), bf16),
            pltpu.VMEM((OWN, WAVE), bf16),
            pltpu.VMEM((SLAB, WAVE), f32),
            pltpu.VMEM((SLAB, WAVE), f32),
            pltpu.VMEM((SLAB, 2 * NX * WAVE), bf16),
            pltpu.VMEM((2 * NX, WAVE, 2 * NX * WAVE), bf16),
            pltpu.VMEM((2 * NX, 64, 2 * NX * WAVE), bf16),
            pltpu.VMEM((2 * NX, 64, 2 * NX * WAVE), bf16),
            pltpu.VMEM((2 * NX, NX, 64, 2 * WAVE), bf16),
            pltpu.VMEM((2 * NX, 64, 2 * WAVE), bf16),
            pltpu.VMEM((8, 64, 2 * WAVE), bf16),
            dma((3,)),
            dma((3,)),
            dma((2,)),
            dma((2,)),
            dma((NX,)),
            dma((NX,)),
            dma((NX,)),
            dma((NX,)),
            dma((2 * NX,)),
            dma((2 * NX,)),
            dma((2 * NX, NX)),
            dma((2 * NX, NX)),
            dma((2 * NX,)),
            dma((8,)),
            dma,
        ],
        compiler_params=pltpu.CompilerParams(
            collective_id=0, has_side_effects=True, vmem_limit_bytes=48 << 20
        ),
        name="chebyshev_filter",
    )(wavefunctions, cell_hamiltonian, cell_nodes, expand, expand_t)


def solution(mesh):
    placed = (P("dom", "band"), P("dom", None, None), P("dom", None), P("dom"))
    return jax.shard_map(
        shards,
        mesh=mesh,
        in_specs=placed,
        out_specs=(P("dom", "band"), P("dom", "band"), P("dom", "band")),
        check_vma=False,
    )
```

```python
import jax
import jax.numpy as jnp
import numpy as np
from jax import lax
from jax.experimental import pallas as pl
from jax.experimental.pallas import tpu as pltpu
from jax.sharding import PartitionSpec as P

CX, CY, CZ = 2, 4, 4
LINE = 4 * CX + 1
COL = 4 * CY + 1
PLANE = LINE * COL
OWN = 4 * CZ * PLANE
FACE_PAD = 160
GRID = OWN + FACE_PAD
TOTAL = 2688
RUN = 5 * LINE
RUN_PAD = 48
PAIR = 5 * RUN_PAD
PAIRS = CY * CZ
LAYER = 4 * PLANE
SLAB = 768
EARLY = SLAB - FACE_PAD
ACROSS = EARLY + 16
NX = 4
WAVE = 128
SORTED = 2560

filter_center = 1.0
filter_half = 1.5

f32 = jnp.float32
bf16 = jnp.bfloat16
MESH = pl.DeviceIdType.MESH


def expansion():
    e = np.zeros((PAIR, 2 * 128), np.float32)
    for k in range(5):
        for j in range(5):
            for x in range(LINE):
                for cell in range(CX):
                    i = x - 4 * cell
                    if 0 <= i < 5:
                        e[RUN_PAD * k + LINE * j + x, 128 * cell + i + 5 * j + 25 * k] = 1
    return e


def kernel(
    w_ref,
    h_ref,
    nodes_ref,
    e_ref,
    et_ref,
    filtered_ref,
    sums_ref,
    w32,
    h32,
    ident,
    order,
    start,
    section,
    total,
    pairs,
    face_out,
    face_in,
    back_out,
    back_in,
    corner,
    edge_out,
    edge_in,
    slabs,
    waves,
    compact,
    restored,
    piece,
    image,
    right,
    gram,
    from_core,
    half,
    from_x,
    quarter,
    final,
    face_s,
    face_r,
    back_s,
    back_r,
    corner_s,
    corner_r,
    edge_s,
    edge_r,
    x_s,
    x_r,
    y_s,
    y_r,
    core_s,
    core_r,
    red_s,
    red_r,
    fin_s,
    fin_r,
    out_s,
):
    d = lax.axis_index("dom")
    b = lax.axis_index("band")
    n_dom = lax.axis_size("dom")
    chip = lax.div(d, 2)
    core = lax.rem(d, 2)
    x = lax.div(b, 2)
    yh = lax.rem(b, 2)
    yl = lax.rem(chip, 2)
    prev = lax.rem(d + n_dom - 1, n_dom)
    succ = lax.rem(d + 1, n_dom)
    mate = (2 * chip + 1 - core, b)
    across = (d, 2 * x + 1 - yh)

    next_layer = (jnp.where(x == NX - 1, succ, d), 2 * lax.rem(x + 1, NX) + yh)

    def along_x(xx):
        return (d, 2 * xx + yh)

    def other_chip(cc):
        return (2 * cc + core, b)

    barrier = pltpu.get_barrier_semaphore()
    greeted = [(prev, b), (succ, b), mate, across, next_layer]
    greeted += [along_x(lax.rem(x + off, NX)) for off in range(1, NX)]
    greeted += [other_chip(lax.rem(chip + off, 8)) for off in range(1, 8)]
    for device in greeted:
        pl.semaphore_signal(barrier, inc=1, device_id=device, device_id_type=MESH)

    def face_copy(n):
        return pltpu.make_async_remote_copy(
            src_ref=face_out.at[n],
            dst_ref=face_in.at[n],
            send_sem=face_s.at[n],
            recv_sem=face_r.at[n],
            device_id=(prev, b),
            device_id_type=MESH,
        )

    def back_copy(n):
        return pltpu.make_async_remote_copy(
            src_ref=back_out.at[n],
            dst_ref=back_in.at[n],
            send_sem=back_s.at[n],
            recv_sem=back_r.at[n],
            device_id=(succ, b),
            device_id_type=MESH,
        )

    once = 1 + lax.div(d, n_dom)

    def apart(body):
        def step(i, carry):
            body()
            return carry

        lax.fori_loop(0, once, step, 0)

    def send_face(n, field):
        face_out[n] = field[0:FACE_PAD, :].astype(bf16)
        face_copy(n).start()

    def take_face(n, field):
        face_copy(n).wait_recv()

        @apart
        def _():
            field[OWN:GRID, :] = face_in[n].astype(f32)

    corner_copy = pltpu.make_async_remote_copy(
        src_ref=pairs.at[pl.ds(PAIRS - CY, CY), pl.ds(4 * RUN_PAD, RUN_PAD)],
        dst_ref=corner,
        send_sem=corner_s,
        recv_sem=corner_r,
        device_id=(succ, b),
        device_id_type=MESH,
    )

    def add_pair(block, base, source, target, used=range(5), kept=range(5)):
        rows = []
        for k in range(5):
            if k in used:
                rows.append(source[base + PLANE * k : base + PLANE * k + RUN_PAD, :].astype(bf16))
            else:
                rows.append(jnp.zeros((RUN_PAD, WAVE), bf16))
        rows.append(jnp.zeros((16, WAVE), bf16))
        result = jnp.dot(block, jnp.concatenate(rows, axis=0), preferred_element_type=f32)
        for k in kept:
            at = base + PLANE * k
            target[at : at + RUN_PAD, :] += result[RUN_PAD * k : RUN_PAD * (k + 1)]

    def add_layer(cz, source, target, **which):
        for cy in range(CY):
            base = LAYER * cz + 4 * LINE * cy
            add_pair(pairs[CY * cz + cy], base, source, target, **which)

    w32[...] = w_ref[...].astype(f32)
    start[OWN:GRID, :] = jnp.zeros((FACE_PAD, WAVE), f32)
    section[OWN:GRID, :] = jnp.zeros((FACE_PAD, WAVE), f32)

    def gather_layer(cz, carry):
        cleared = pl.ds(pl.multiple_of(TOTAL // CZ * cz, 8), TOTAL // CZ)
        for n in range(2):
            total[n, cleared, :] = jnp.zeros((TOTAL // CZ, WAVE), f32)
        for k in range(4):
            for q in range(COL):
                cy = min(q // 4, CY - 1)
                for p in range(LINE):
                    cx = min(p // 4, CX - 1)
                    slot = (p - 4 * cx) + 5 * (q - 4 * cy) + 25 * k
                    node = nodes_ref[cz, cy * CX + cx, slot]
                    row = cz * LAYER + k * PLANE + q * LINE + p
                    start[pl.ds(row, 1), :] = w32[pl.ds(node, 1), :]
                    ident[pl.ds(row, 1), :] = jnp.full((1, WAVE), node, jnp.int32)
        return carry

    lax.fori_loop(0, CZ, gather_layer, 0)
    pl.semaphore_wait(barrier, len(greeted))
    send_face(0, start)

    @apart
    def _():
        h32[:, 125:WAVE] = jnp.zeros((125 * CX * PAIRS, WAVE - 125), f32)
        h32[:, 0:125] = h_ref[...].astype(f32)

    def make_pairs(p):
        sides = []
        for cell in range(CX):
            cells = [
                h32[pl.ds(CX * (p + q) + cell, 125, stride=CX * PAIRS), :].astype(bf16)
                for q in range(2)
            ]
            side = jnp.dot(
                e_ref[:, 128 * cell : 128 * cell + 125],
                jnp.concatenate(cells, axis=1),
                preferred_element_type=f32,
            )
            sides.append(side.astype(bf16))
        for q in range(2):
            both = [side[:, 128 * q : 128 * (q + 1)] for side in sides]
            block = jnp.dot(
                jnp.concatenate(both, axis=1), et_ref[...], preferred_element_type=f32
            )
            pairs[p + q] = block.astype(bf16)

    def below(n, field):
        add_layer(CZ - 1, field, total.at[n], used=range(4))

        @apart
        def _():
            back_out[n] = total[n, OWN:GRID, :]
            back_copy(n).start()

    def inner(n, field):
        for cz in range(CZ - 1):
            add_layer(cz, field, total.at[n])

    def above(n, field):
        take_face(n, field)
        add_layer(CZ - 1, field, total.at[n], used=(4,), kept=range(4))

    def shared(n, field):
        for cy in range(CY):
            at = 4 * LINE * cy
            rows = jnp.concatenate(
                [
                    jnp.zeros((4 * RUN_PAD, WAVE), bf16),
                    field[at : at + RUN_PAD, :].astype(bf16),
                    jnp.zeros((16, WAVE), bf16),
                ],
                axis=0,
            )
            result = jnp.dot(corner[cy], rows, preferred_element_type=f32)
            total[n, at : at + RUN_PAD, :] += result

    def take_back(n):
        back_copy(n).wait_recv()

        @apart
        def _():
            total[n, 0:FACE_PAD, :] += back_in[n]

    def to_section(lo, hi):
        value = (total[0, lo:hi, :] - filter_center * start[lo:hi, :]) * (1.0 / filter_half)
        section[lo:hi, :] = value.astype(bf16).astype(f32)

    def to_filtered(lo, hi):
        value = (total[1, lo:hi, :] - filter_center * section[lo:hi, :]) * (2.0 / filter_half)
        value = (value - start[lo:hi, :]).astype(bf16)
        compact[lo:hi, :] = value
        start[lo:hi, :] = value.astype(f32)

    make_pairs(PAIRS - 4)
    make_pairs(PAIRS - 2)
    corner_copy.start()
    below(0, start)
    for p in range(0, PAIRS - 4, 2):
        make_pairs(p)
    inner(0, start)
    corner_copy.wait_recv()
    shared(0, start)
    take_back(0)

    @apart
    def _():
        to_section(0, FACE_PAD)
        send_face(1, section)

    above(0, start)
    apart(lambda: to_section(FACE_PAD, OWN))
    below(1, section)
    inner(1, section)
    shared(1, section)
    above(1, section)
    take_back(1)

    @apart
    def _():
        to_filtered(0, OWN)
        send_face(2, start)

    x_rows = (pl.ds(0, EARLY), pl.ds(EARLY, FACE_PAD))
    y_rows = (pl.ds(0, EARLY), pl.ds(EARLY, ACROSS - EARLY))

    def x_copy(j, part):
        return pltpu.make_async_remote_copy(
            src_ref=slabs.at[j, x_rows[part]],
            dst_ref=waves.at[x, x_rows[part]],
            send_sem=x_s.at[part, j],
            recv_sem=x_r.at[part, x],
            device_id=along_x(j),
            device_id_type=MESH,
        )

    def x_arrival(xx, part):
        return pltpu.make_async_remote_copy(
            src_ref=slabs.at[0, x_rows[part]],
            dst_ref=waves.at[xx, x_rows[part]],
            send_sem=x_s.at[part, 0],
            recv_sem=x_r.at[part, xx],
            device_id=along_x(xx),
            device_id_type=MESH,
        )

    def y_copy(xx, part):
        return pltpu.make_async_remote_copy(
            src_ref=waves.at[xx, y_rows[part]],
            dst_ref=waves.at[NX + xx, y_rows[part]],
            send_sem=y_s.at[part, xx],
            recv_sem=y_r.at[part, xx],
            device_id=across,
            device_id_type=MESH,
        )

    def fill_slab(j, part):
        lo, hi = (0, EARLY) if part == 0 else (EARLY, SLAB)
        value = start[LAYER * j + lo : LAYER * j + hi, :].astype(bf16)
        slabs[j, lo:hi, :] = value

        @pl.when(x == j)
        def _():
            waves[j, lo:hi, :] = value
            y_copy(j, part).start()

    def send_slabs(layers, part):
        for j in layers:
            fill_slab(j, part)
        for off in (1, 3, 2):
            jj = lax.rem(x + off, NX)
            wanted = jj == layers[0]
            for j in layers[1:]:
                wanted = jnp.logical_or(wanted, jj == j)

            @pl.when(wanted)
            def _():
                x_copy(jj, part).start()

    send_slabs((0, 1, 2, 3), 0)
    send_slabs((0, 1, 2), 1)

    compact[OWN:SORTED, :] = jnp.zeros((SORTED - OWN, WAVE), bf16)
    ident[OWN:SORTED, :] = jnp.full((SORTED - OWN, WAVE), -1, jnp.int32)
    for t in range(SORTED // WAVE):
        order[:, WAVE * t : WAVE * (t + 1)] = ident[WAVE * t : WAVE * (t + 1), :].T[:8]

    def restore(lo, hi):
        rows = lax.broadcasted_iota(jnp.int32, (hi - lo, 256), 0) + lo
        value = jnp.zeros((hi - lo, WAVE), f32)
        for t in range(SORTED // 256):
            here = jnp.broadcast_to(order[0:1, 256 * t : 256 * (t + 1)], (hi - lo, 256))
            hit = jnp.where(rows == here, 1.0, 0.0).astype(bf16)
            value += jnp.dot(hit, compact[256 * t : 256 * (t + 1), :], preferred_element_type=f32)
        restored[lo:hi, :] = value.astype(bf16)

    def out_copy():
        return pltpu.make_async_copy(restored, filtered_ref, out_s)

    own_rows = lax.broadcasted_iota(jnp.int32, (SLAB, WAVE), 0) < LAYER

    def take_piece(xx):
        @apart
        def _():
            piece[...] = waves[xx].astype(f32)

        def clear(i, carry):
            rows = pl.ds(pl.multiple_of(112 * i, 8), 112)
            image[rows, :] = jnp.zeros((112, WAVE), f32)
            return carry

        lax.fori_loop(0, (SLAB + 16) // 112, clear, 0)

        for cy in range(CY):
            add_pair(pairs[CY * x + cy], 4 * LINE * cy, piece, image)

        @apart
        def _():
            at = pl.multiple_of(2 * WAVE * xx, 2 * WAVE)
            right[:, pl.ds(at, WAVE)] = jnp.where(own_rows, piece[...], 0.0).astype(bf16)
            right[:, pl.ds(at + WAVE, WAVE)] = image[0:SLAB, :].astype(bf16)
            edge_out[xx] = image[LAYER : LAYER + FACE_PAD, :].astype(bf16)

    def pass_on(off, part):
        xx = lax.rem(x + off, NX)
        x_arrival(xx, part).wait_recv()
        y_copy(xx, part).start()

    restore(0, 640)
    take_face(2, start)
    send_slabs((NX - 1,), 1)
    pass_on(1, 0)
    pass_on(3, 0)
    take_piece(x)
    pass_on(1, 1)
    pass_on(2, 0)
    take_piece(lax.rem(x + 1, NX))
    pass_on(3, 1)
    take_piece(lax.rem(x + 3, NX))
    pass_on(2, 1)
    take_piece(lax.rem(x + 2, NX))

    edge_copy = pltpu.make_async_remote_copy(
        src_ref=edge_out,
        dst_ref=edge_in,
        send_sem=edge_s,
        recv_sem=edge_r,
        device_id=next_layer,
        device_id_type=MESH,
    )
    edge_copy.start()

    def complete_image():
        edge_copy.wait_recv()
        last = lax.broadcasted_iota(jnp.int32, (16, WAVE), 0) < LAYER - EARLY
        for xx in range(NX):
            at = 2 * WAVE * xx + WAVE
            value = right[0:FACE_PAD, at : at + WAVE].astype(f32) + edge_in[xx].astype(f32)
            right[0:FACE_PAD, at : at + WAVE] = value.astype(bf16)
            value = right[EARLY:ACROSS, at : at + WAVE].astype(f32)
            right[EARLY:ACROSS, at : at + WAVE] = jnp.where(last, value, 0.0).astype(bf16)

    keep = pl.multiple_of(64 * core, 64)
    give = pl.multiple_of(64 * (1 - core), 64)

    def core_copy(t):
        return pltpu.make_async_remote_copy(
            src_ref=gram.at[t, pl.ds(give, 64)],
            dst_ref=from_core.at[t],
            send_sem=core_s.at[t],
            recv_sem=core_r.at[t],
            device_id=mate,
            device_id_type=MESH,
        )

    def block_of(xx):
        return pl.ds(pl.multiple_of(2 * WAVE * xx, 2 * WAVE), 2 * WAVE)

    def red_copy(t, xx):
        return pltpu.make_async_remote_copy(
            src_ref=half.at[t, :, block_of(xx)],
            dst_ref=from_x.at[t, x],
            send_sem=red_s.at[t, xx],
            recv_sem=red_r.at[t, x],
            device_id=along_x(xx),
            device_id_type=MESH,
        )

    def red_arrival(t, xx):
        return pltpu.make_async_remote_copy(
            src_ref=half.at[t, :, block_of(xx)],
            dst_ref=from_x.at[t, xx],
            send_sem=red_s.at[t, xx],
            recv_sem=red_r.at[t, xx],
            device_id=along_x(xx),
            device_id_type=MESH,
        )

    def target_chip(t):
        band_side = jnp.where(t < NX, yh, 1 - yh)
        return 2 * lax.rem(t, NX) + band_side

    def fin_copy(t):
        return pltpu.make_async_remote_copy(
            src_ref=quarter.at[t],
            dst_ref=final.at[chip],
            send_sem=fin_s.at[t],
            recv_sem=fin_r.at[chip],
            device_id=other_chip(target_chip(t)),
            device_id_type=MESH,
        )

    def fin_arrival(cc):
        return pltpu.make_async_remote_copy(
            src_ref=quarter.at[0],
            dst_ref=final.at[cc],
            send_sem=fin_s.at[0],
            recv_sem=fin_r.at[cc],
            device_id=other_chip(cc),
            device_id_type=MESH,
        )

    def multiply(t, rows):
        gram[t] = lax.dot_general(
            waves[t, 0:rows, :],
            right[0:rows, :],
            (((0,), (0,)), ((), ())),
            preferred_element_type=f32,
        ).astype(bf16)
        core_copy(t).start()

    def sum_core(t):
        core_copy(t).wait_recv()
        value = gram[t, pl.ds(keep, 64), :].astype(f32) + from_core[t].astype(f32)
        half[t] = value.astype(bf16)
        for off in range(1, NX):
            red_copy(t, lax.rem(x + off, NX)).start()

    def sum_x(t):
        value = half[t, :, block_of(x)].astype(f32)
        for off in range(1, NX):
            xx = lax.rem(x + off, NX)
            red_arrival(t, xx).wait_recv()
            value += from_x[t, xx].astype(f32)
        quarter[t] = value.astype(bf16)
        away = target_chip(t) != chip

        @pl.when(away)
        def _():
            fin_copy(t).start()

        @pl.when(jnp.logical_not(away))
        def _():
            final[chip] = quarter[t]

    def own_round(t, carry):
        multiply(t, SLAB)

        @pl.when(t >= 1)
        def _():
            sum_core(t - 1)

        return carry

    lax.fori_loop(0, NX, own_round, 0)
    sum_core(NX - 1)
    for lo, hi in ((640, 1280), (1280, 1920), (1920, OWN)):
        restore(lo, hi)
    out_copy().start()
    apart(complete_image)

    def arrival_order(i):
        off = jnp.where(i == 2, 3, jnp.where(i == 3, 2, i))
        return NX + lax.rem(x + off, NX)

    def other_round(i, carry):
        t = arrival_order(i)
        for part in range(2):
            y_copy(t - NX, part).wait_recv()
        multiply(t, ACROSS)

        @pl.when(i >= 1)
        def _():
            sum_core(arrival_order(i - 1))

        sum_x(i)
        return carry

    lax.fori_loop(0, NX, other_round, 0)
    sum_core(arrival_order(NX - 1))

    def last_round(i, carry):
        sum_x(arrival_order(i))
        return carry

    lax.fori_loop(0, NX, last_round, 0)

    for cc in range(8):

        @pl.when(chip != cc)
        def _():
            fin_arrival(cc).wait_recv()

    result = final[0].astype(f32)
    for cc in range(1, 8):
        result += final[cc].astype(f32)
    sums_ref[...] = result

    for n in range(3):
        face_copy(n).wait_send()
    for n in range(2):
        back_copy(n).wait_send()
    corner_copy.wait_send()
    edge_copy.wait_send()
    for part in range(2):
        for j in range(NX):

            @pl.when(x != j)
            def _():
                x_copy(j, part).wait_send()

            y_copy(j, part).wait_send()

    def drain(t, carry):
        core_copy(t).wait_send()
        for off in range(1, NX):
            red_copy(t, lax.rem(x + off, NX)).wait_send()

        @pl.when(target_chip(t) != chip)
        def _():
            fin_copy(t).wait_send()

        return carry

    lax.fori_loop(0, 2 * NX, drain, 0)
    out_copy().wait()


def shards(wavefunctions, cell_hamiltonian, cell_nodes, face_nodes):
    e = expansion()
    expand = jnp.asarray(e, bf16)
    expand_t = jnp.asarray(np.pad(e.T, ((0, 0), (0, 256 - PAIR))), bf16)
    vmem = pl.BlockSpec(memory_space=pltpu.VMEM)
    dma = pltpu.SemaphoreType.DMA
    by_row = cell_hamiltonian.transpose(1, 0, 2).reshape(125 * CX * PAIRS, 125)
    filtered, sums = pl.pallas_call(
        kernel,
        out_shape=(
            jax.ShapeDtypeStruct((OWN, WAVE), bf16),
            jax.ShapeDtypeStruct((64, 2 * WAVE), f32),
        ),
        in_specs=[vmem, vmem, pl.BlockSpec(memory_space=pltpu.SMEM), vmem, vmem],
        out_specs=(pl.BlockSpec(memory_space=pl.ANY), vmem),
        scratch_shapes=[
            pltpu.VMEM((OWN, WAVE), f32),
            pltpu.VMEM((125 * CX * PAIRS, WAVE), f32),
            pltpu.VMEM((SORTED, WAVE), jnp.int32),
            pltpu.VMEM((8, SORTED), jnp.int32),
            pltpu.VMEM((GRID, WAVE), f32),
            pltpu.VMEM((GRID, WAVE), f32),
            pltpu.VMEM((2, TOTAL, WAVE), f32),
            pltpu.VMEM((PAIRS, PAIR, 256), bf16),
            pltpu.VMEM((3, FACE_PAD, WAVE), bf16),
            pltpu.VMEM((3, FACE_PAD, WAVE), bf16),
            pltpu.VMEM((2, FACE_PAD, WAVE), f32),
            pltpu.VMEM((2, FACE_PAD, WAVE), f32),
            pltpu.VMEM((CY, RUN_PAD, 256), bf16),
            pltpu.VMEM((NX, FACE_PAD, WAVE), bf16),
            pltpu.VMEM((NX, FACE_PAD, WAVE), bf16),
            pltpu.VMEM((NX, SLAB, WAVE), bf16),
            pltpu.VMEM((2 * NX, SLAB, WAVE), bf16),
            pltpu.VMEM((SORTED, WAVE), bf16),
            pltpu.VMEM((OWN, WAVE), bf16),
            pltpu.VMEM((SLAB, WAVE), f32),
            pltpu.VMEM((SLAB + 16, WAVE), f32),
            pltpu.VMEM((SLAB, 2 * NX * WAVE), bf16),
            pltpu.VMEM((2 * NX, WAVE, 2 * NX * WAVE), bf16),
            pltpu.VMEM((2 * NX, 64, 2 * NX * WAVE), bf16),
            pltpu.VMEM((2 * NX, 64, 2 * NX * WAVE), bf16),
            pltpu.VMEM((2 * NX, NX, 64, 2 * WAVE), bf16),
            pltpu.VMEM((2 * NX, 64, 2 * WAVE), bf16),
            pltpu.VMEM((8, 64, 2 * WAVE), bf16),
            dma((3,)),
            dma((3,)),
            dma((2,)),
            dma((2,)),
            dma,
            dma,
            dma,
            dma,
            dma((2, NX)),
            dma((2, NX)),
            dma((2, NX)),
            dma((2, NX)),
            dma((2 * NX,)),
            dma((2 * NX,)),
            dma((2 * NX, NX)),
            dma((2 * NX, NX)),
            dma((2 * NX,)),
            dma((8,)),
            dma,
        ],
        compiler_params=pltpu.CompilerParams(
            collective_id=0, has_side_effects=True, vmem_limit_bytes=48 << 20
        ),
        name="chebyshev_filter",
    )(wavefunctions, by_row, cell_nodes.reshape(CZ, CX * CY, 125), expand, expand_t)
    nodes = lax.axis_size("dom") * OWN
    return filtered, sums[:, :WAVE] / nodes, sums[:, WAVE:] / nodes


def solution(mesh):
    placed = (P("dom", "band"), P("dom", None, None), P("dom", None), P("dom"))
    return jax.shard_map(
        shards,
        mesh=mesh,
        in_specs=placed,
        out_specs=(P("dom", "band"), P("dom", "band"), P("dom", "band")),
        check_vma=False,
    )
```

```python
import jax
import jax.numpy as jnp
import numpy as np
from jax import lax
from jax.experimental import pallas as pl
from jax.experimental.pallas import tpu as pltpu
from jax.sharding import PartitionSpec as P

CX, CY, CZ = 2, 4, 4
LINE = 4 * CX + 1
COL = 4 * CY + 1
PLANE = LINE * COL
OWN = 4 * CZ * PLANE
FACE_PAD = 160
GRID = OWN + FACE_PAD
TOTAL = 2688
RUN = 5 * LINE
RUN_PAD = 48
PAIR = 5 * RUN_PAD
PAIRS = CY * CZ
LAYER = 4 * PLANE
SLAB = 768
EARLY = SLAB - FACE_PAD
ACROSS = EARLY + 16
NX = 4
WAVE = 128
SORTED = 2560

filter_center = 1.0
filter_half = 1.5

f32 = jnp.float32
bf16 = jnp.bfloat16
MESH = pl.DeviceIdType.MESH


def expansion():
    e = np.zeros((PAIR, 2 * 128), np.float32)
    for k in range(5):
        for j in range(5):
            for x in range(LINE):
                for cell in range(CX):
                    i = x - 4 * cell
                    if 0 <= i < 5:
                        e[RUN_PAD * k + LINE * j + x, 128 * cell + i + 5 * j + 25 * k] = 1
    return e


def kernel(
    w_hbm,
    h_hbm,
    nodes_hbm,
    e_hbm,
    et_hbm,
    filtered_ref,
    sums_ref,
    w_ref,
    h_ref,
    nodes_ref,
    e_ref,
    et_ref,
    w32,
    h32,
    ident,
    order,
    start,
    section,
    total,
    pairs,
    face_out,
    face_in,
    back_out,
    back_in,
    corner,
    edge_out,
    edge_in,
    slabs,
    waves,
    compact,
    restored,
    piece,
    image,
    right,
    gram,
    from_core,
    half,
    from_x,
    quarter,
    final,
    face_s,
    face_r,
    back_s,
    back_r,
    corner_s,
    corner_r,
    edge_s,
    edge_r,
    x_s,
    x_r,
    y_s,
    y_r,
    core_s,
    core_r,
    red_s,
    red_r,
    fin_s,
    fin_r,
    out_s,
    in_s,
):
    d = lax.axis_index("dom")
    b = lax.axis_index("band")
    n_dom = lax.axis_size("dom")
    chip = lax.div(d, 2)
    core = lax.rem(d, 2)
    x = lax.div(b, 2)
    yh = lax.rem(b, 2)
    yl = lax.rem(chip, 2)
    prev = lax.rem(d + n_dom - 1, n_dom)
    succ = lax.rem(d + 1, n_dom)
    mate = (2 * chip + 1 - core, b)
    across = (d, 2 * x + 1 - yh)

    next_layer = (jnp.where(x == NX - 1, succ, d), 2 * lax.rem(x + 1, NX) + yh)

    def along_x(xx):
        return (d, 2 * xx + yh)

    def other_chip(cc):
        return (2 * cc + core, b)

    loads = [
        pltpu.make_async_copy(source, target, in_s.at[n])
        for n, (source, target) in enumerate(
            (
                (nodes_hbm, nodes_ref),
                (w_hbm, w_ref),
                (h_hbm, h_ref),
                (e_hbm, e_ref),
                (et_hbm, et_ref),
            )
        )
    ]
    for load in loads:
        load.start()

    barrier = pltpu.get_barrier_semaphore()
    greeted = [(prev, b), (succ, b), mate, across, next_layer]
    greeted += [along_x(lax.rem(x + off, NX)) for off in range(1, NX)]
    greeted += [other_chip(lax.rem(chip + off, 8)) for off in range(1, 8)]
    for device in greeted:
        pl.semaphore_signal(barrier, inc=1, device_id=device, device_id_type=MESH)

    def face_copy(n):
        return pltpu.make_async_remote_copy(
            src_ref=face_out.at[n],
            dst_ref=face_in.at[n],
            send_sem=face_s.at[n],
            recv_sem=face_r.at[n],
            device_id=(prev, b),
            device_id_type=MESH,
        )

    def back_copy(n):
        return pltpu.make_async_remote_copy(
            src_ref=back_out.at[n],
            dst_ref=back_in.at[n],
            send_sem=back_s.at[n],
            recv_sem=back_r.at[n],
            device_id=(succ, b),
            device_id_type=MESH,
        )

    once = 1 + lax.div(d, n_dom)

    def apart(body):
        def step(i, carry):
            body()
            return carry

        lax.fori_loop(0, once, step, 0)

    def send_face(n, field):
        face_out[n] = field[0:FACE_PAD, :].astype(bf16)
        face_copy(n).start()

    def take_face(n, field):
        face_copy(n).wait_recv()

        @apart
        def _():
            field[OWN:GRID, :] = face_in[n].astype(f32)

    corner_copy = pltpu.make_async_remote_copy(
        src_ref=pairs.at[pl.ds(PAIRS - CY, CY), pl.ds(4 * RUN_PAD, RUN_PAD)],
        dst_ref=corner,
        send_sem=corner_s,
        recv_sem=corner_r,
        device_id=(succ, b),
        device_id_type=MESH,
    )

    def add_pair(block, base, source, target, used=range(5), kept=range(5)):
        rows = []
        for k in range(5):
            if k in used:
                rows.append(source[base + PLANE * k : base + PLANE * k + RUN_PAD, :].astype(bf16))
            else:
                rows.append(jnp.zeros((RUN_PAD, WAVE), bf16))
        rows.append(jnp.zeros((16, WAVE), bf16))
        result = jnp.dot(block, jnp.concatenate(rows, axis=0), preferred_element_type=f32)
        for k in kept:
            at = base + PLANE * k
            target[at : at + RUN_PAD, :] += result[RUN_PAD * k : RUN_PAD * (k + 1)]

    def add_layer(cz, source, target, **which):
        for cy in range(CY):
            base = LAYER * cz + 4 * LINE * cy
            add_pair(pairs[CY * cz + cy], base, source, target, **which)

    loads[0].wait()
    loads[1].wait()
    w32[...] = w_ref[...].astype(f32)
    start[OWN:GRID, :] = jnp.zeros((FACE_PAD, WAVE), f32)
    section[OWN:GRID, :] = jnp.zeros((FACE_PAD, WAVE), f32)

    def gather_layer(cz, carry):
        cleared = pl.ds(pl.multiple_of(TOTAL // CZ * cz, 8), TOTAL // CZ)
        for n in range(2):
            total[n, cleared, :] = jnp.zeros((TOTAL // CZ, WAVE), f32)
        for k in range(4):
            for q in range(COL):
                cy = min(q // 4, CY - 1)
                for p in range(LINE):
                    cx = min(p // 4, CX - 1)
                    slot = (p - 4 * cx) + 5 * (q - 4 * cy) + 25 * k
                    node = nodes_ref[cz, cy * CX + cx, slot]
                    row = cz * LAYER + k * PLANE + q * LINE + p
                    start[pl.ds(row, 1), :] = w32[pl.ds(node, 1), :]
        return carry

    lax.fori_loop(0, CZ, gather_layer, 0)
    for load in loads[2:]:
        load.wait()
    pl.semaphore_wait(barrier, len(greeted))
    send_face(0, start)

    @apart
    def _():
        h32[:, 125:WAVE] = jnp.zeros((125 * CX * PAIRS, WAVE - 125), f32)
        h32[:, 0:125] = h_ref[...].astype(f32)

    def make_pairs(p):
        sides = []
        for cell in range(CX):
            cells = [
                h32[pl.ds(CX * (p + q) + cell, 125, stride=CX * PAIRS), :].astype(bf16)
                for q in range(2)
            ]
            side = jnp.dot(
                e_ref[:, 128 * cell : 128 * cell + 125],
                jnp.concatenate(cells, axis=1),
                preferred_element_type=f32,
            )
            sides.append(side.astype(bf16))
        for q in range(2):
            both = [side[:, 128 * q : 128 * (q + 1)] for side in sides]
            block = jnp.dot(
                jnp.concatenate(both, axis=1), et_ref[...], preferred_element_type=f32
            )
            pairs[p + q] = block.astype(bf16)

    def below(n, field):
        add_layer(CZ - 1, field, total.at[n], used=range(4))

        @apart
        def _():
            back_out[n] = total[n, OWN:GRID, :]
            back_copy(n).start()

    def inner(n, field):
        for cz in range(CZ - 1):
            add_layer(cz, field, total.at[n])

    def above(n, field):
        take_face(n, field)
        add_layer(CZ - 1, field, total.at[n], used=(4,), kept=range(4))

    def shared(n, field):
        for cy in range(CY):
            at = 4 * LINE * cy
            rows = jnp.concatenate(
                [
                    jnp.zeros((4 * RUN_PAD, WAVE), bf16),
                    field[at : at + RUN_PAD, :].astype(bf16),
                    jnp.zeros((16, WAVE), bf16),
                ],
                axis=0,
            )
            result = jnp.dot(corner[cy], rows, preferred_element_type=f32)
            total[n, at : at + RUN_PAD, :] += result

    def take_back(n):
        back_copy(n).wait_recv()

        @apart
        def _():
            total[n, 0:FACE_PAD, :] += back_in[n]

    def to_section(lo, hi):
        value = (total[0, lo:hi, :] - filter_center * start[lo:hi, :]) * (1.0 / filter_half)
        section[lo:hi, :] = value.astype(bf16).astype(f32)

    def to_filtered(lo, hi):
        value = (total[1, lo:hi, :] - filter_center * section[lo:hi, :]) * (2.0 / filter_half)
        value = (value - start[lo:hi, :]).astype(bf16)
        compact[lo:hi, :] = value
        start[lo:hi, :] = value.astype(f32)

    make_pairs(PAIRS - 4)
    make_pairs(PAIRS - 2)
    corner_copy.start()
    below(0, start)
    for p in range(0, PAIRS - 4, 2):
        make_pairs(p)
    inner(0, start)
    corner_copy.wait_recv()
    shared(0, start)
    take_back(0)

    @apart
    def _():
        to_section(0, FACE_PAD)
        send_face(1, section)

    above(0, start)
    apart(lambda: to_section(FACE_PAD, OWN))
    below(1, section)
    inner(1, section)
    shared(1, section)
    above(1, section)

    def number_layer(cz, carry):
        for k in range(4):
            for q in range(COL):
                cy = min(q // 4, CY - 1)
                for p in range(LINE):
                    cx = min(p // 4, CX - 1)
                    slot = (p - 4 * cx) + 5 * (q - 4 * cy) + 25 * k
                    node = nodes_ref[cz, cy * CX + cx, slot]
                    row = cz * LAYER + k * PLANE + q * LINE + p
                    ident[pl.ds(row, 1), :] = jnp.full((1, WAVE), node, jnp.int32)
        return carry

    lax.fori_loop(0, CZ, number_layer, 0)
    take_back(1)

    @apart
    def _():
        to_filtered(0, OWN)
        send_face(2, start)

    x_rows = (pl.ds(0, EARLY), pl.ds(EARLY, FACE_PAD))
    y_rows = (pl.ds(0, EARLY), pl.ds(EARLY, ACROSS - EARLY))

    def x_copy(j, part):
        return pltpu.make_async_remote_copy(
            src_ref=slabs.at[j, x_rows[part]],
            dst_ref=waves.at[x, x_rows[part]],
            send_sem=x_s.at[part, j],
            recv_sem=x_r.at[part, x],
            device_id=along_x(j),
            device_id_type=MESH,
        )

    def x_arrival(xx, part):
        return pltpu.make_async_remote_copy(
            src_ref=slabs.at[0, x_rows[part]],
            dst_ref=waves.at[xx, x_rows[part]],
            send_sem=x_s.at[part, 0],
            recv_sem=x_r.at[part, xx],
            device_id=along_x(xx),
            device_id_type=MESH,
        )

    def y_copy(xx, part):
        return pltpu.make_async_remote_copy(
            src_ref=waves.at[xx, y_rows[part]],
            dst_ref=waves.at[NX + xx, y_rows[part]],
            send_sem=y_s.at[part, xx],
            recv_sem=y_r.at[part, xx],
            device_id=across,
            device_id_type=MESH,
        )

    def fill_slab(j, part):
        lo, hi = (0, EARLY) if part == 0 else (EARLY, SLAB)
        value = start[LAYER * j + lo : LAYER * j + hi, :].astype(bf16)
        slabs[j, lo:hi, :] = value

        @pl.when(x == j)
        def _():
            waves[j, lo:hi, :] = value
            y_copy(j, part).start()

    def send_slabs(layers, part):
        for j in layers:
            fill_slab(j, part)
        for off in (1, 3, 2):
            jj = lax.rem(x + off, NX)
            wanted = jj == layers[0]
            for j in layers[1:]:
                wanted = jnp.logical_or(wanted, jj == j)

            @pl.when(wanted)
            def _():
                x_copy(jj, part).start()

    send_slabs((0, 1, 2, 3), 0)
    send_slabs((0, 1, 2), 1)

    compact[OWN:SORTED, :] = jnp.zeros((SORTED - OWN, WAVE), bf16)
    ident[OWN:SORTED, :] = jnp.full((SORTED - OWN, WAVE), -1, jnp.int32)
    for t in range(SORTED // WAVE):
        order[:, WAVE * t : WAVE * (t + 1)] = ident[WAVE * t : WAVE * (t + 1), :].T[:8]

    def restore(lo, hi):
        rows = lax.broadcasted_iota(jnp.int32, (hi - lo, 256), 0) + lo
        value = jnp.zeros((hi - lo, WAVE), f32)
        for t in range(SORTED // 256):
            here = jnp.broadcast_to(order[0:1, 256 * t : 256 * (t + 1)], (hi - lo, 256))
            hit = jnp.where(rows == here, 1.0, 0.0).astype(bf16)
            value += jnp.dot(hit, compact[256 * t : 256 * (t + 1), :], preferred_element_type=f32)
        restored[lo:hi, :] = value.astype(bf16)

    def out_copy():
        return pltpu.make_async_copy(restored, filtered_ref, out_s)

    own_rows = lax.broadcasted_iota(jnp.int32, (SLAB, WAVE), 0) < LAYER

    def take_piece(xx):
        @apart
        def _():
            piece[...] = waves[xx].astype(f32)

        def clear(i, carry):
            rows = pl.ds(pl.multiple_of(112 * i, 8), 112)
            image[rows, :] = jnp.zeros((112, WAVE), f32)
            return carry

        lax.fori_loop(0, (SLAB + 16) // 112, clear, 0)

        for cy in range(CY):
            add_pair(pairs[CY * x + cy], 4 * LINE * cy, piece, image)

        @apart
        def _():
            at = pl.multiple_of(2 * WAVE * xx, 2 * WAVE)
            right[:, pl.ds(at, WAVE)] = jnp.where(own_rows, piece[...], 0.0).astype(bf16)
            right[:, pl.ds(at + WAVE, WAVE)] = image[0:SLAB, :].astype(bf16)
            edge_out[xx] = image[LAYER : LAYER + FACE_PAD, :].astype(bf16)
            edge_copy(xx).start()

    def pass_on(off, part):
        xx = lax.rem(x + off, NX)
        x_arrival(xx, part).wait_recv()
        y_copy(xx, part).start()

    def edge_copy(xx):
        return pltpu.make_async_remote_copy(
            src_ref=edge_out.at[xx],
            dst_ref=edge_in.at[xx],
            send_sem=edge_s.at[xx],
            recv_sem=edge_r.at[xx],
            device_id=next_layer,
            device_id_type=MESH,
        )

    restore(0, 640)
    take_face(2, start)
    send_slabs((NX - 1,), 1)
    pass_on(1, 0)
    pass_on(3, 0)
    take_piece(x)
    pass_on(2, 0)
    pass_on(1, 1)
    take_piece(lax.rem(x + 1, NX))
    pass_on(3, 1)
    take_piece(lax.rem(x + 3, NX))
    pass_on(2, 1)
    take_piece(lax.rem(x + 2, NX))

    def complete_image():
        for xx in range(NX):
            edge_copy(xx).wait_recv()
        last = lax.broadcasted_iota(jnp.int32, (16, WAVE), 0) < LAYER - EARLY
        for xx in range(NX):
            at = 2 * WAVE * xx + WAVE
            value = right[0:FACE_PAD, at : at + WAVE].astype(f32) + edge_in[xx].astype(f32)
            right[0:FACE_PAD, at : at + WAVE] = value.astype(bf16)
            value = right[EARLY:ACROSS, at : at + WAVE].astype(f32)
            right[EARLY:ACROSS, at : at + WAVE] = jnp.where(last, value, 0.0).astype(bf16)

    keep = pl.multiple_of(64 * core, 64)
    give = pl.multiple_of(64 * (1 - core), 64)

    def core_copy(t):
        return pltpu.make_async_remote_copy(
            src_ref=gram.at[t, pl.ds(give, 64)],
            dst_ref=from_core.at[t],
            send_sem=core_s.at[t],
            recv_sem=core_r.at[t],
            device_id=mate,
            device_id_type=MESH,
        )

    def block_of(xx):
        return pl.ds(pl.multiple_of(2 * WAVE * xx, 2 * WAVE), 2 * WAVE)

    def red_copy(t, xx):
        return pltpu.make_async_remote_copy(
            src_ref=half.at[t, :, block_of(xx)],
            dst_ref=from_x.at[t, x],
            send_sem=red_s.at[t, xx],
            recv_sem=red_r.at[t, x],
            device_id=along_x(xx),
            device_id_type=MESH,
        )

    def red_arrival(t, xx):
        return pltpu.make_async_remote_copy(
            src_ref=half.at[t, :, block_of(xx)],
            dst_ref=from_x.at[t, xx],
            send_sem=red_s.at[t, xx],
            recv_sem=red_r.at[t, xx],
            device_id=along_x(xx),
            device_id_type=MESH,
        )

    def target_chip(t):
        band_side = jnp.where(t < NX, yh, 1 - yh)
        return 2 * lax.rem(t, NX) + band_side

    def fin_copy(t):
        return pltpu.make_async_remote_copy(
            src_ref=quarter.at[t],
            dst_ref=final.at[chip],
            send_sem=fin_s.at[t],
            recv_sem=fin_r.at[chip],
            device_id=other_chip(target_chip(t)),
            device_id_type=MESH,
        )

    def fin_arrival(cc):
        return pltpu.make_async_remote_copy(
            src_ref=quarter.at[0],
            dst_ref=final.at[cc],
            send_sem=fin_s.at[0],
            recv_sem=fin_r.at[cc],
            device_id=other_chip(cc),
            device_id_type=MESH,
        )

    def multiply(t, rows):
        gram[t] = lax.dot_general(
            waves[t, 0:rows, :],
            right[0:rows, :],
            (((0,), (0,)), ((), ())),
            preferred_element_type=f32,
        ).astype(bf16)
        core_copy(t).start()

    def sum_core(t):
        core_copy(t).wait_recv()
        value = gram[t, pl.ds(keep, 64), :].astype(f32) + from_core[t].astype(f32)
        half[t] = value.astype(bf16)
        for off in range(1, NX):
            red_copy(t, lax.rem(x + off, NX)).start()

    def sum_x(t):
        value = half[t, :, block_of(x)].astype(f32)
        for off in range(1, NX):
            xx = lax.rem(x + off, NX)
            red_arrival(t, xx).wait_recv()
            value += from_x[t, xx].astype(f32)
        quarter[t] = value.astype(bf16)
        away = target_chip(t) != chip

        @pl.when(away)
        def _():
            fin_copy(t).start()

        @pl.when(jnp.logical_not(away))
        def _():
            final[chip] = quarter[t]

    def own_round(t, carry):
        multiply(t, SLAB)

        @pl.when(t >= 1)
        def _():
            sum_core(t - 1)

        return carry

    lax.fori_loop(0, NX, own_round, 0)
    sum_core(NX - 1)
    for lo, hi in ((640, 1280), (1280, 1920), (1920, OWN)):
        restore(lo, hi)
    out_copy().start()
    apart(complete_image)

    def arrival_order(i):
        off = jnp.where(i == 2, 3, jnp.where(i == 3, 2, i))
        return NX + lax.rem(x + off, NX)

    def other_round(i, carry):
        t = arrival_order(i)
        for part in range(2):
            y_copy(t - NX, part).wait_recv()
        multiply(t, ACROSS)

        @pl.when(i >= 1)
        def _():
            sum_core(arrival_order(i - 1))

        sum_x(i)
        return carry

    lax.fori_loop(0, NX, other_round, 0)
    sum_core(arrival_order(NX - 1))

    def last_round(i, carry):
        sum_x(arrival_order(i))
        return carry

    lax.fori_loop(0, NX, last_round, 0)

    for cc in range(8):

        @pl.when(chip != cc)
        def _():
            fin_arrival(cc).wait_recv()

    result = final[0].astype(f32)
    for cc in range(1, 8):
        result += final[cc].astype(f32)
    sums_ref[...] = result * (1.0 / (n_dom * OWN))

    for n in range(3):
        face_copy(n).wait_send()
    for n in range(2):
        back_copy(n).wait_send()
    corner_copy.wait_send()
    for xx in range(NX):
        edge_copy(xx).wait_send()
    for part in range(2):
        for j in range(NX):

            @pl.when(x != j)
            def _():
                x_copy(j, part).wait_send()

            y_copy(j, part).wait_send()

    def drain(t, carry):
        core_copy(t).wait_send()
        for off in range(1, NX):
            red_copy(t, lax.rem(x + off, NX)).wait_send()

        @pl.when(target_chip(t) != chip)
        def _():
            fin_copy(t).wait_send()

        return carry

    lax.fori_loop(0, 2 * NX, drain, 0)
    out_copy().wait()


def finish(filtered_ref, sums_ref, out_ref, corr_ref, proj_ref, sums, held, sem):
    whole = pltpu.make_async_copy(filtered_ref, held, sem.at[0])
    whole.start()
    load = pltpu.make_async_copy(sums_ref, sums, sem.at[1])
    load.start()
    load.wait()
    stores = [
        pltpu.make_async_copy(sums.at[:, pl.ds(WAVE * n, WAVE)], target, sem.at[2 + n])
        for n, target in enumerate((corr_ref, proj_ref))
    ]
    for store in stores:
        store.start()
    whole.wait()
    back = pltpu.make_async_copy(held, out_ref, sem.at[4])
    back.start()
    for store in stores:
        store.wait()
    back.wait()


def shards(wavefunctions, cell_hamiltonian, cell_nodes, face_nodes):
    e = expansion()
    expand = jnp.asarray(e, bf16)
    expand_t = jnp.asarray(np.pad(e.T, ((0, 0), (0, 256 - PAIR))), bf16)
    vmem = pl.BlockSpec(memory_space=pltpu.VMEM)
    dma = pltpu.SemaphoreType.DMA
    by_row = cell_hamiltonian.transpose(1, 0, 2).reshape(125 * CX * PAIRS, 125)
    filtered, sums = pl.pallas_call(
        kernel,
        out_shape=(
            jax.ShapeDtypeStruct((OWN, WAVE), bf16),
            jax.ShapeDtypeStruct((64, 2 * WAVE), f32),
        ),
        in_specs=[pl.BlockSpec(memory_space=pltpu.HBM)] * 5,
        out_specs=(pl.BlockSpec(memory_space=pl.ANY), vmem),
        scratch_shapes=[
            pltpu.VMEM((OWN, WAVE), bf16),
            pltpu.VMEM((125 * CX * PAIRS, 125), bf16),
            pltpu.SMEM((CZ, CX * CY, 125), jnp.int32),
            pltpu.VMEM((PAIR, 256), bf16),
            pltpu.VMEM((256, 256), bf16),
            pltpu.VMEM((OWN, WAVE), f32),
            pltpu.VMEM((125 * CX * PAIRS, WAVE), f32),
            pltpu.VMEM((SORTED, WAVE), jnp.int32),
            pltpu.VMEM((8, SORTED), jnp.int32),
            pltpu.VMEM((GRID, WAVE), f32),
            pltpu.VMEM((GRID, WAVE), f32),
            pltpu.VMEM((2, TOTAL, WAVE), f32),
            pltpu.VMEM((PAIRS, PAIR, 256), bf16),
            pltpu.VMEM((3, FACE_PAD, WAVE), bf16),
            pltpu.VMEM((3, FACE_PAD, WAVE), bf16),
            pltpu.VMEM((2, FACE_PAD, WAVE), f32),
            pltpu.VMEM((2, FACE_PAD, WAVE), f32),
            pltpu.VMEM((CY, RUN_PAD, 256), bf16),
            pltpu.VMEM((NX, FACE_PAD, WAVE), bf16),
            pltpu.VMEM((NX, FACE_PAD, WAVE), bf16),
            pltpu.VMEM((NX, SLAB, WAVE), bf16),
            pltpu.VMEM((2 * NX, SLAB, WAVE), bf16),
            pltpu.VMEM((SORTED, WAVE), bf16),
            pltpu.VMEM((OWN, WAVE), bf16),
            pltpu.VMEM((SLAB, WAVE), f32),
            pltpu.VMEM((SLAB + 16, WAVE), f32),
            pltpu.VMEM((SLAB, 2 * NX * WAVE), bf16),
            pltpu.VMEM((2 * NX, WAVE, 2 * NX * WAVE), bf16),
            pltpu.VMEM((2 * NX, 64, 2 * NX * WAVE), bf16),
            pltpu.VMEM((2 * NX, 64, 2 * NX * WAVE), bf16),
            pltpu.VMEM((2 * NX, NX, 64, 2 * WAVE), bf16),
            pltpu.VMEM((2 * NX, 64, 2 * WAVE), bf16),
            pltpu.VMEM((8, 64, 2 * WAVE), bf16),
            dma((3,)),
            dma((3,)),
            dma((2,)),
            dma((2,)),
            dma,
            dma,
            dma((NX,)),
            dma((NX,)),
            dma((2, NX)),
            dma((2, NX)),
            dma((2, NX)),
            dma((2, NX)),
            dma((2 * NX,)),
            dma((2 * NX,)),
            dma((2 * NX, NX)),
            dma((2 * NX, NX)),
            dma((2 * NX,)),
            dma((8,)),
            dma,
            dma((5,)),
        ],
        compiler_params=pltpu.CompilerParams(
            collective_id=0, has_side_effects=True, vmem_limit_bytes=63 << 20
        ),
        name="chebyshev_filter",
    )(wavefunctions, by_row, cell_nodes.reshape(CZ, CX * CY, 125), expand, expand_t)
    hbm = pl.BlockSpec(memory_space=pltpu.HBM)
    return pl.pallas_call(
        finish,
        out_shape=(
            jax.ShapeDtypeStruct((OWN, WAVE), bf16),
            jax.ShapeDtypeStruct((64, WAVE), f32),
            jax.ShapeDtypeStruct((64, WAVE), f32),
        ),
        in_specs=[hbm, hbm],
        out_specs=(hbm, hbm, hbm),
        scratch_shapes=[
            pltpu.VMEM((64, 2 * WAVE), f32),
            pltpu.VMEM((OWN, WAVE), bf16),
            dma((5,)),
        ],
        compiler_params=pltpu.CompilerParams(vmem_limit_bytes=63 << 20),
        name="finish",
    )(filtered, sums)


def solution(mesh):
    placed = (P("dom", "band"), P("dom", None, None), P("dom", None), P("dom"))
    return jax.shard_map(
        shards,
        mesh=mesh,
        in_specs=placed,
        out_specs=(P("dom", "band"), P("dom", "band"), P("dom", "band")),
        check_vma=False,
    )
```

```python
import jax
import jax.numpy as jnp
import numpy as np
from jax import lax
from jax.experimental import pallas as pl
from jax.experimental.pallas import tpu as pltpu
from jax.sharding import PartitionSpec as P

CX, CY, CZ = 2, 4, 4
LINE = 4 * CX + 1
COL = 4 * CY + 1
PLANE = LINE * COL
OWN = 4 * CZ * PLANE
FACE_PAD = 160
GRID = OWN + FACE_PAD
TOTAL = 2688
RUN = 5 * LINE
RUN_PAD = 48
PAIR = 5 * RUN_PAD
PAIRS = CY * CZ
LAYER = 4 * PLANE
SLAB = 768
EARLY = SLAB - FACE_PAD
ACROSS = EARLY + 16
HELD = ACROSS + FACE_PAD
READY = 3 * LAYER
PITCH = CX * PAIRS + 1
NX = 4
WAVE = 128
SORTED = 2560

filter_center = 1.0
filter_half = 1.5

f32 = jnp.float32
bf16 = jnp.bfloat16
MESH = pl.DeviceIdType.MESH


def expansion():
    e = np.zeros((PAIR, 2 * 128), np.float32)
    for k in range(5):
        for j in range(5):
            for x in range(LINE):
                for cell in range(CX):
                    i = x - 4 * cell
                    if 0 <= i < 5:
                        e[RUN_PAD * k + LINE * j + x, 128 * cell + i + 5 * j + 25 * k] = 1
    return e


def kernel(
    w_hbm,
    h_hbm,
    nodes_hbm,
    e_hbm,
    et_hbm,
    filtered_ref,
    sums_ref,
    w_ref,
    h_ref,
    nodes_ref,
    e_ref,
    et_ref,
    w32,
    h32,
    ident,
    order,
    start,
    section,
    total,
    pairs,
    face_out,
    face_in,
    back_out,
    back_in,
    corner,
    edge_out,
    edge_in,
    slabs,
    waves,
    compact,
    restored,
    piece,
    image,
    right,
    gram,
    from_core,
    half,
    from_x,
    from_z,
    quarter,
    final,
    face_s,
    face_r,
    back_s,
    back_r,
    corner_s,
    corner_r,
    edge_s,
    edge_r,
    x_s,
    x_r,
    y_s,
    y_r,
    core_s,
    core_r,
    red_s,
    red_r,
    z_s,
    z_r,
    fin_s,
    fin_r,
    out_s,
    in_s,
):
    d = lax.axis_index("dom")
    b = lax.axis_index("band")
    n_dom = lax.axis_size("dom")
    chip = lax.div(d, 2)
    core = lax.rem(d, 2)
    x = lax.div(b, 2)
    yh = lax.rem(b, 2)
    yl = lax.rem(chip, 2)
    prev = lax.rem(d + n_dom - 1, n_dom)
    succ = lax.rem(d + 1, n_dom)
    mate = (2 * chip + 1 - core, b)
    across = (d, 2 * x + 1 - yh)

    next_layer = (jnp.where(x == NX - 1, succ, d), 2 * lax.rem(x + 1, NX) + yh)

    def along_x(xx):
        return (d, 2 * xx + yh)

    def other_chip(cc):
        return (2 * cc + core, b)

    loads = [
        pltpu.make_async_copy(source, target, in_s.at[n])
        for n, (source, target) in enumerate(
            (
                (nodes_hbm, nodes_ref),
                (w_hbm, w_ref),
                (h_hbm, h_ref),
                (e_hbm, e_ref),
                (et_hbm, et_ref),
            )
        )
    ]
    for load in loads:
        load.start()

    barrier = pltpu.get_barrier_semaphore()
    greeted = [(prev, b), (succ, b), mate, across, next_layer]
    greeted += [along_x(lax.rem(x + off, NX)) for off in range(1, NX)]
    greeted += [other_chip(lax.rem(chip + off, 8)) for off in range(1, 8)]
    for device in greeted:
        pl.semaphore_signal(barrier, inc=1, device_id=device, device_id_type=MESH)

    def face_copy(n):
        return pltpu.make_async_remote_copy(
            src_ref=face_out.at[n],
            dst_ref=face_in.at[n],
            send_sem=face_s.at[n],
            recv_sem=face_r.at[n],
            device_id=(prev, b),
            device_id_type=MESH,
        )

    def back_copy(n):
        return pltpu.make_async_remote_copy(
            src_ref=back_out.at[n],
            dst_ref=back_in.at[n],
            send_sem=back_s.at[n],
            recv_sem=back_r.at[n],
            device_id=(succ, b),
            device_id_type=MESH,
        )

    once = 1 + lax.div(d, n_dom)

    def apart(body):
        def step(i, carry):
            body()
            return carry

        lax.fori_loop(0, once, step, 0)

    def send_face(n, field):
        face_out[n] = field[0:FACE_PAD, :].astype(bf16)
        face_copy(n).start()

    def take_face(n, field):
        face_copy(n).wait_recv()

        @apart
        def _():
            field[OWN:GRID, :] = face_in[n].astype(f32)

    corner_copy = pltpu.make_async_remote_copy(
        src_ref=pairs.at[pl.ds(PAIRS - CY, CY), pl.ds(4 * RUN_PAD, RUN_PAD)],
        dst_ref=corner,
        send_sem=corner_s,
        recv_sem=corner_r,
        device_id=(succ, b),
        device_id_type=MESH,
    )

    def add_pair(block, base, source, target, used=range(5), kept=range(5)):
        rows = []
        for k in range(5):
            if k in used:
                rows.append(source[base + PLANE * k : base + PLANE * k + RUN_PAD, :].astype(bf16))
            else:
                rows.append(jnp.zeros((RUN_PAD, WAVE), bf16))
        rows.append(jnp.zeros((16, WAVE), bf16))
        result = jnp.dot(block, jnp.concatenate(rows, axis=0), preferred_element_type=f32)
        for k in kept:
            at = base + PLANE * k
            target[at : at + RUN_PAD, :] += result[RUN_PAD * k : RUN_PAD * (k + 1)]

    def add_layer(cz, source, target, **which):
        for cy in range(CY):
            base = LAYER * cz + 4 * LINE * cy
            add_pair(pairs[CY * cz + cy], base, source, target, **which)

    loads[0].wait()
    loads[1].wait()
    w32[...] = w_ref[...].astype(f32)
    start[OWN:GRID, :] = jnp.zeros((FACE_PAD, WAVE), f32)
    section[OWN:GRID, :] = jnp.zeros((FACE_PAD, WAVE), f32)

    def gather_layer(cz, carry):
        cleared = pl.ds(pl.multiple_of(TOTAL // CZ * cz, 8), TOTAL // CZ)
        for n in range(2):
            total[n, cleared, :] = jnp.zeros((TOTAL // CZ, WAVE), f32)
        for k in range(4):
            for q in range(COL):
                cy = min(q // 4, CY - 1)
                for p in range(LINE):
                    cx = min(p // 4, CX - 1)
                    slot = (p - 4 * cx) + 5 * (q - 4 * cy) + 25 * k
                    node = nodes_ref[cz, cy * CX + cx, slot]
                    row = cz * LAYER + k * PLANE + q * LINE + p
                    start[pl.ds(row, 1), :] = w32[pl.ds(node, 1), :]
        return carry

    lax.fori_loop(0, CZ, gather_layer, 0)
    for load in loads[2:]:
        load.wait()
    pl.semaphore_wait(barrier, len(greeted))
    send_face(0, start)

    @apart
    def _():
        def fill(i, carry):
            for u in range(5):
                row = 5 * i + u
                here = pl.ds(PITCH * row, CX * PAIRS)
                there = pl.ds(pl.multiple_of(CX * PAIRS * row, CX * PAIRS), CX * PAIRS)
                h32[here, 125:WAVE] = jnp.zeros((CX * PAIRS, WAVE - 125), f32)
                h32[here, 0:125] = h_ref[there, :].astype(f32)
            return carry

        lax.fori_loop(0, 25, fill, 0)

    def make_pairs(p):
        sides = []
        for cell in range(CX):
            cells = [
                h32[pl.ds(CX * (p + q) + cell, 125, stride=PITCH), :].astype(bf16)
                for q in range(2)
            ]
            side = jnp.dot(
                e_ref[:, 128 * cell : 128 * cell + 125],
                jnp.concatenate(cells, axis=1),
                preferred_element_type=f32,
            )
            sides.append(side.astype(bf16))
        for q in range(2):
            both = [side[:, 128 * q : 128 * (q + 1)] for side in sides]
            block = jnp.dot(
                jnp.concatenate(both, axis=1), et_ref[...], preferred_element_type=f32
            )
            pairs[p + q] = block.astype(bf16)

    def below(n, field):
        add_layer(CZ - 1, field, total.at[n], used=range(4))

        @apart
        def _():
            back_out[n] = total[n, OWN:GRID, :]
            back_copy(n).start()

    def inner(n, field):
        for cz in range(CZ - 1):
            add_layer(cz, field, total.at[n])

    def above(n, field):
        take_face(n, field)
        add_layer(CZ - 1, field, total.at[n], used=(4,), kept=range(4))

    def shared(n, field):
        for cy in range(CY):
            at = 4 * LINE * cy
            rows = jnp.concatenate(
                [
                    jnp.zeros((4 * RUN_PAD, WAVE), bf16),
                    field[at : at + RUN_PAD, :].astype(bf16),
                    jnp.zeros((16, WAVE), bf16),
                ],
                axis=0,
            )
            result = jnp.dot(corner[cy], rows, preferred_element_type=f32)
            total[n, at : at + RUN_PAD, :] += result

    def take_back(n):
        back_copy(n).wait_recv()

        @apart
        def _():
            total[n, 0:FACE_PAD, :] += back_in[n]

    def to_section(lo, hi):
        value = (total[0, lo:hi, :] - filter_center * start[lo:hi, :]) * (1.0 / filter_half)
        section[lo:hi, :] = value.astype(bf16).astype(f32)

    def to_filtered(lo, hi):
        value = (total[1, lo:hi, :] - filter_center * section[lo:hi, :]) * (2.0 / filter_half)
        value = (value - start[lo:hi, :]).astype(bf16)
        start[lo:hi, :] = value.astype(f32)

    make_pairs(PAIRS - 4)
    make_pairs(PAIRS - 2)
    corner_copy.start()
    below(0, start)
    for p in range(0, PAIRS - 4, 2):
        make_pairs(p)
    inner(0, start)
    corner_copy.wait_recv()
    shared(0, start)
    take_back(0)

    @apart
    def _():
        to_section(0, FACE_PAD)
        send_face(1, section)

    above(0, start)
    apart(lambda: to_section(FACE_PAD, OWN))
    below(1, section)
    inner(1, section)
    shared(1, section)
    x_rows = (pl.ds(0, ACROSS), pl.ds(ACROSS, FACE_PAD))

    def x_copy(j, part):
        return pltpu.make_async_remote_copy(
            src_ref=slabs.at[j, x_rows[part]],
            dst_ref=waves.at[x, x_rows[part]],
            send_sem=x_s.at[part, j],
            recv_sem=x_r.at[part, x],
            device_id=along_x(j),
            device_id_type=MESH,
        )

    def x_arrival(xx, part):
        return pltpu.make_async_remote_copy(
            src_ref=slabs.at[0, x_rows[part]],
            dst_ref=waves.at[xx, x_rows[part]],
            send_sem=x_s.at[part, 0],
            recv_sem=x_r.at[part, xx],
            device_id=along_x(xx),
            device_id_type=MESH,
        )

    def y_copy(xx):
        return pltpu.make_async_remote_copy(
            src_ref=waves.at[xx, pl.ds(0, ACROSS)],
            dst_ref=waves.at[NX + xx, pl.ds(0, ACROSS)],
            send_sem=y_s.at[xx],
            recv_sem=y_r.at[xx],
            device_id=across,
            device_id_type=MESH,
        )

    def keep_compact():
        compact[0:OWN, :] = start[0:OWN, :].astype(bf16)

    def fill_slab(j, part):
        base = LAYER * j
        if part == 0:
            last = lax.broadcasted_iota(jnp.int32, (ACROSS - EARLY, WAVE), 0) < LAYER - EARLY
            value = jnp.concatenate(
                [
                    start[base : base + EARLY, :],
                    jnp.where(last, start[base + EARLY : base + ACROSS, :], 0.0),
                ],
                axis=0,
            ).astype(bf16)
            lo, hi = 0, ACROSS
        else:
            value = start[base + EARLY : base + SLAB, :].astype(bf16)
            lo, hi = ACROSS, HELD
        slabs[j, lo:hi, :] = value

        @pl.when(x == j)
        def _():
            waves[j, lo:hi, :] = value
            if part == 0:
                y_copy(j).start()

    def send_slabs(layers, part, offs):
        for off in offs:
            jj = lax.rem(x + off, NX)
            wanted = jj == layers[0]
            for j in layers[1:]:
                wanted = jnp.logical_or(wanted, jj == j)

            @pl.when(wanted)
            def _():
                x_copy(jj, part).start()

    apart(lambda: to_filtered(FACE_PAD, READY))
    for j, part in ((1, 0), (2, 0), (1, 1)):
        fill_slab(j, part)
    send_slabs((1, 2), 0, (1, 3, 2))
    send_slabs((1,), 1, (1, 3, 2))

    above(1, section)

    def number_layer(cz, carry):
        for k in range(4):
            for q in range(COL):
                cy = min(q // 4, CY - 1)
                for p in range(LINE):
                    cx = min(p // 4, CX - 1)
                    slot = (p - 4 * cx) + 5 * (q - 4 * cy) + 25 * k
                    node = nodes_ref[cz, cy * CX + cx, slot]
                    row = cz * LAYER + k * PLANE + q * LINE + p
                    ident[pl.ds(row, 1), :] = jnp.full((1, WAVE), node, jnp.int32)
        return carry

    lax.fori_loop(0, CZ, number_layer, 0)
    take_back(1)

    @apart
    def _():
        to_filtered(0, FACE_PAD)
        to_filtered(READY, OWN)
        send_face(2, start)

    for j, part in ((0, 0), (3, 0), (0, 1), (2, 1)):
        fill_slab(j, part)
    send_slabs((0, 3), 0, (1, 3, 2))
    send_slabs((0, 2), 1, (1, 3, 2))
    apart(keep_compact)

    compact[OWN:SORTED, :] = jnp.zeros((SORTED - OWN, WAVE), bf16)
    ident[OWN:SORTED, :] = jnp.full((SORTED - OWN, WAVE), -1, jnp.int32)
    for t in range(SORTED // WAVE):
        order[:, WAVE * t : WAVE * (t + 1)] = ident[WAVE * t : WAVE * (t + 1), :].T[:8]

    def restore(lo, hi):
        rows = lax.broadcasted_iota(jnp.int32, (hi - lo, 256), 0) + lo
        value = jnp.zeros((hi - lo, WAVE), f32)
        for t in range(SORTED // 256):
            here = jnp.broadcast_to(order[0:1, 256 * t : 256 * (t + 1)], (hi - lo, 256))
            hit = jnp.where(rows == here, 1.0, 0.0).astype(bf16)
            value += jnp.dot(hit, compact[256 * t : 256 * (t + 1), :], preferred_element_type=f32)
        restored[lo:hi, :] = value.astype(bf16)

    def out_copy():
        return pltpu.make_async_copy(restored, filtered_ref, out_s)

    own_rows = lax.broadcasted_iota(jnp.int32, (SLAB, WAVE), 0) < LAYER

    def take_piece(xx):
        @apart
        def _():
            piece[0:EARLY, :] = waves[xx, 0:EARLY, :].astype(f32)
            piece[EARLY:SLAB, :] = waves[xx, ACROSS:HELD, :].astype(f32)

        def clear(i, carry):
            rows = pl.ds(pl.multiple_of(112 * i, 8), 112)
            image[rows, :] = jnp.zeros((112, WAVE), f32)
            return carry

        lax.fori_loop(0, (SLAB + 16) // 112, clear, 0)

        for cy in range(CY):
            add_pair(pairs[CY * x + cy], 4 * LINE * cy, piece, image)

        @apart
        def _():
            at = pl.multiple_of(2 * WAVE * xx, 2 * WAVE)
            right[:, pl.ds(at, WAVE)] = jnp.where(own_rows, piece[...], 0.0).astype(bf16)
            right[:, pl.ds(at + WAVE, WAVE)] = image[0:SLAB, :].astype(bf16)
            edge_out[xx] = image[LAYER : LAYER + FACE_PAD, :].astype(bf16)
            edge_copy(xx).start()

    def pass_on(off, part):
        xx = lax.rem(x + off, NX)
        x_arrival(xx, part).wait_recv()
        if part == 0:
            y_copy(xx).start()

    def edge_copy(xx):
        return pltpu.make_async_remote_copy(
            src_ref=edge_out.at[xx],
            dst_ref=edge_in.at[xx],
            send_sem=edge_s.at[xx],
            recv_sem=edge_r.at[xx],
            device_id=next_layer,
            device_id_type=MESH,
        )

    restore(0, 640)
    take_face(2, start)
    fill_slab(NX - 1, 1)
    send_slabs((NX - 1,), 1, (1, 3, 2))
    pass_on(1, 0)
    pass_on(3, 0)
    take_piece(x)
    pass_on(2, 0)
    pass_on(1, 1)
    take_piece(lax.rem(x + 1, NX))
    pass_on(3, 1)
    take_piece(lax.rem(x + 3, NX))
    pass_on(2, 1)
    take_piece(lax.rem(x + 2, NX))

    def complete_image():
        for xx in range(NX):
            edge_copy(xx).wait_recv()
        last = lax.broadcasted_iota(jnp.int32, (16, WAVE), 0) < LAYER - EARLY
        for xx in range(NX):
            at = 2 * WAVE * xx + WAVE
            value = right[0:FACE_PAD, at : at + WAVE].astype(f32) + edge_in[xx].astype(f32)
            right[0:FACE_PAD, at : at + WAVE] = value.astype(bf16)
            value = right[EARLY:ACROSS, at : at + WAVE].astype(f32)
            right[EARLY:ACROSS, at : at + WAVE] = jnp.where(last, value, 0.0).astype(bf16)

    keep = pl.multiple_of(64 * core, 64)
    give = pl.multiple_of(64 * (1 - core), 64)

    def core_copy(t):
        return pltpu.make_async_remote_copy(
            src_ref=gram.at[t, pl.ds(give, 64)],
            dst_ref=from_core.at[t],
            send_sem=core_s.at[t],
            recv_sem=core_r.at[t],
            device_id=mate,
            device_id_type=MESH,
        )

    def block_of(xx):
        return pl.ds(pl.multiple_of(2 * WAVE * xx, 2 * WAVE), 2 * WAVE)

    def red_copy(t, xx):
        return pltpu.make_async_remote_copy(
            src_ref=half.at[t, :, block_of(xx)],
            dst_ref=from_x.at[t, x],
            send_sem=red_s.at[t, xx],
            recv_sem=red_r.at[t, x],
            device_id=along_x(xx),
            device_id_type=MESH,
        )

    def red_arrival(t, xx):
        return pltpu.make_async_remote_copy(
            src_ref=half.at[t, :, block_of(xx)],
            dst_ref=from_x.at[t, xx],
            send_sem=red_s.at[t, xx],
            recv_sem=red_r.at[t, xx],
            device_id=along_x(xx),
            device_id_type=MESH,
        )

    def target_chip(t):
        band_side = jnp.where(t < NX, yh, 1 - yh)
        return 2 * lax.rem(t, NX) + band_side

    def fin_copy(t):
        return pltpu.make_async_remote_copy(
            src_ref=quarter.at[t],
            dst_ref=final.at[chip],
            send_sem=fin_s.at[t],
            recv_sem=fin_r.at[chip],
            device_id=other_chip(target_chip(t)),
            device_id_type=MESH,
        )

    def fin_arrival(cc):
        return pltpu.make_async_remote_copy(
            src_ref=quarter.at[0],
            dst_ref=final.at[cc],
            send_sem=fin_s.at[0],
            recv_sem=fin_r.at[cc],
            device_id=other_chip(cc),
            device_id_type=MESH,
        )

    z = lax.div(chip, 2)

    def z_copy(t):
        return pltpu.make_async_remote_copy(
            src_ref=half.at[t],
            dst_ref=from_z.at[z],
            send_sem=z_s.at[t],
            recv_sem=z_r.at[z],
            device_id=other_chip(2 * t + yl),
            device_id_type=MESH,
        )

    def z_arrival(zz):
        return pltpu.make_async_remote_copy(
            src_ref=half.at[zz],
            dst_ref=from_z.at[zz],
            send_sem=z_s.at[zz],
            recv_sem=z_r.at[zz],
            device_id=other_chip(2 * zz + yl),
            device_id_type=MESH,
        )

    def multiply(t, own):
        if own:
            left = jnp.concatenate([waves[t, 0:EARLY, :], waves[t, ACROSS:HELD, :]], axis=0)
            factor = right[...]
        else:
            left = waves[t, 0:ACROSS, :]
            factor = right[0:ACROSS, :]
        gram[t] = lax.dot_general(
            left, factor, (((0,), (0,)), ((), ())), preferred_element_type=f32
        ).astype(bf16)
        core_copy(t).start()

    def sum_core(t):
        core_copy(t).wait_recv()
        value = gram[t, pl.ds(keep, 64), :].astype(f32) + from_core[t].astype(f32)
        half[t] = value.astype(bf16)

    def send_x(t):
        for off in range(1, NX):
            red_copy(t, lax.rem(x + off, NX)).start()

    def sum_z():
        value = half[z].astype(f32)
        for off in range(1, CZ):
            zz = lax.rem(z + off, CZ)
            z_arrival(zz).wait_recv()
            value += from_z[zz].astype(f32)
        half[z] = value.astype(bf16)
        send_x(z)

    def sum_x(t):
        value = half[t, :, block_of(x)].astype(f32)
        for off in range(1, NX):
            xx = lax.rem(x + off, NX)
            red_arrival(t, xx).wait_recv()
            value += from_x[t, xx].astype(f32)
        quarter[t] = value.astype(bf16)
        away = target_chip(t) != chip

        @pl.when(away)
        def _():
            fin_copy(t).start()

        @pl.when(jnp.logical_not(away))
        def _():
            final[chip] = quarter[t]

    def own_round(t, carry):
        multiply(t, True)
        return carry

    lax.fori_loop(0, NX, own_round, 0)

    def own_sum(t, carry):
        sum_core(t)

        @pl.when(t != z)
        def _():
            z_copy(t).start()

        return carry

    lax.fori_loop(0, NX, own_sum, 0)
    restore(640, 1280)
    restore(1280, 1920)
    apart(complete_image)

    def arrival_order(i):
        off = jnp.where(i == 2, 3, jnp.where(i == 3, 2, i))
        return NX + lax.rem(x + off, NX)

    def other_sum(i):
        sum_core(arrival_order(i))
        send_x(arrival_order(i))

    def other_round(i, carry):
        @pl.when(i >= 1)
        def _():
            other_sum(i - 1)

        t = arrival_order(i)
        y_copy(t - NX).wait_recv()
        multiply(t, False)
        return carry

    lax.fori_loop(0, NX, other_round, 0)
    other_sum(NX - 1)
    sum_z()
    restore(1920, OWN)
    out_copy().start()

    def last_round(i, carry):
        sum_x(arrival_order(i))
        return carry

    lax.fori_loop(0, NX, last_round, 0)
    sum_x(z)

    nodes = n_dom * OWN

    @pl.when(yl == yh)
    def _():
        fin_arrival(2 * z + 1 - yl).wait_recv()
        result = final[2 * z].astype(f32) + final[2 * z + 1].astype(f32)
        sums_ref[...] = result * (1.0 / nodes)

    @pl.when(yl != yh)
    def _():
        for off in range(1, 8):
            fin_arrival(lax.rem(chip + off, 8)).wait_recv()
        result = final[0].astype(f32)
        for cc in range(1, 8):
            result += final[cc].astype(f32)
        sums_ref[...] = result * (1.0 / nodes)

    for n in range(3):
        face_copy(n).wait_send()
    for n in range(2):
        back_copy(n).wait_send()
    corner_copy.wait_send()
    for xx in range(NX):
        edge_copy(xx).wait_send()
    for j in range(NX):
        y_copy(j).wait_send()
    for part in range(2):
        for j in range(NX):

            @pl.when(x != j)
            def _():
                x_copy(j, part).wait_send()


    def drain(t, carry):
        core_copy(t).wait_send()

        @pl.when(jnp.logical_or(t >= NX, t == z))
        def _():
            for off in range(1, NX):
                red_copy(t, lax.rem(x + off, NX)).wait_send()

            @pl.when(target_chip(t) != chip)
            def _():
                fin_copy(t).wait_send()

        @pl.when(jnp.logical_and(t < NX, t != z))
        def _():
            z_copy(t).wait_send()

        return carry

    lax.fori_loop(0, 2 * NX, drain, 0)
    out_copy().wait()


def finish(filtered_ref, sums_ref, out_ref, corr_ref, proj_ref, sums, held, sem):
    chunks = [(640 * n, min(640, OWN - 640 * n)) for n in range(4)]
    loads = [
        pltpu.make_async_copy(
            filtered_ref.at[pl.ds(at, rows)], held.at[pl.ds(at, rows)], sem.at[n]
        )
        for n, (at, rows) in enumerate(chunks)
    ]
    load = pltpu.make_async_copy(sums_ref, sums, sem.at[4])
    load.start()
    for one in loads:
        one.start()
    load.wait()
    stores = [
        pltpu.make_async_copy(sums.at[:, pl.ds(WAVE * n, WAVE)], target, sem.at[5 + n])
        for n, target in enumerate((corr_ref, proj_ref))
    ]
    for store in stores:
        store.start()
    for n, (at, rows) in enumerate(chunks):
        loads[n].wait()
        store = pltpu.make_async_copy(
            held.at[pl.ds(at, rows)], out_ref.at[pl.ds(at, rows)], sem.at[7 + n]
        )
        store.start()
        stores.append(store)
    for store in stores:
        store.wait()


def shards(wavefunctions, cell_hamiltonian, cell_nodes, face_nodes):
    e = expansion()
    expand = jnp.asarray(e, bf16)
    expand_t = jnp.asarray(np.pad(e.T, ((0, 0), (0, 256 - PAIR))), bf16)
    vmem = pl.BlockSpec(memory_space=pltpu.VMEM)
    dma = pltpu.SemaphoreType.DMA
    by_row = cell_hamiltonian.transpose(1, 0, 2).reshape(125 * CX * PAIRS, 125)
    filtered, sums = pl.pallas_call(
        kernel,
        out_shape=(
            jax.ShapeDtypeStruct((OWN, WAVE), bf16),
            jax.ShapeDtypeStruct((64, 2 * WAVE), f32),
        ),
        in_specs=[pl.BlockSpec(memory_space=pltpu.HBM)] * 5,
        out_specs=(pl.BlockSpec(memory_space=pl.ANY), vmem),
        scratch_shapes=[
            pltpu.VMEM((OWN, WAVE), bf16),
            pltpu.VMEM((125 * CX * PAIRS, 125), bf16),
            pltpu.SMEM((CZ, CX * CY, 125), jnp.int32),
            pltpu.VMEM((PAIR, 256), bf16),
            pltpu.VMEM((256, 256), bf16),
            pltpu.VMEM((OWN, WAVE), f32),
            pltpu.VMEM((125 * PITCH + 3, WAVE), f32),
            pltpu.VMEM((SORTED, WAVE), jnp.int32),
            pltpu.VMEM((8, SORTED), jnp.int32),
            pltpu.VMEM((GRID, WAVE), f32),
            pltpu.VMEM((GRID, WAVE), f32),
            pltpu.VMEM((2, TOTAL, WAVE), f32),
            pltpu.VMEM((PAIRS, PAIR, 256), bf16),
            pltpu.VMEM((3, FACE_PAD, WAVE), bf16),
            pltpu.VMEM((3, FACE_PAD, WAVE), bf16),
            pltpu.VMEM((2, FACE_PAD, WAVE), f32),
            pltpu.VMEM((2, FACE_PAD, WAVE), f32),
            pltpu.VMEM((CY, RUN_PAD, 256), bf16),
            pltpu.VMEM((NX, FACE_PAD, WAVE), bf16),
            pltpu.VMEM((NX, FACE_PAD, WAVE), bf16),
            pltpu.VMEM((NX, HELD, WAVE), bf16),
            pltpu.VMEM((2 * NX, HELD, WAVE), bf16),
            pltpu.VMEM((SORTED, WAVE), bf16),
            pltpu.VMEM((OWN, WAVE), bf16),
            pltpu.VMEM((SLAB, WAVE), f32),
            pltpu.VMEM((SLAB + 16, WAVE), f32),
            pltpu.VMEM((SLAB, 2 * NX * WAVE), bf16),
            pltpu.VMEM((2 * NX, WAVE, 2 * NX * WAVE), bf16),
            pltpu.VMEM((2 * NX, 64, 2 * NX * WAVE), bf16),
            pltpu.VMEM((2 * NX, 64, 2 * NX * WAVE), bf16),
            pltpu.VMEM((2 * NX, NX, 64, 2 * WAVE), bf16),
            pltpu.VMEM((CZ, 64, 2 * NX * WAVE), bf16),
            pltpu.VMEM((2 * NX, 64, 2 * WAVE), bf16),
            pltpu.VMEM((8, 64, 2 * WAVE), bf16),
            dma((3,)),
            dma((3,)),
            dma((2,)),
            dma((2,)),
            dma,
            dma,
            dma((NX,)),
            dma((NX,)),
            dma((2, NX)),
            dma((2, NX)),
            dma((NX,)),
            dma((NX,)),
            dma((2 * NX,)),
            dma((2 * NX,)),
            dma((2 * NX, NX)),
            dma((2 * NX, NX)),
            dma((CZ,)),
            dma((CZ,)),
            dma((2 * NX,)),
            dma((8,)),
            dma,
            dma((5,)),
        ],
        compiler_params=pltpu.CompilerParams(
            collective_id=0, has_side_effects=True, vmem_limit_bytes=63 << 20
        ),
        name="chebyshev_filter",
    )(wavefunctions, by_row, cell_nodes.reshape(CZ, CX * CY, 125), expand, expand_t)
    hbm = pl.BlockSpec(memory_space=pltpu.HBM)
    return pl.pallas_call(
        finish,
        out_shape=(
            jax.ShapeDtypeStruct((OWN, WAVE), bf16),
            jax.ShapeDtypeStruct((64, WAVE), f32),
            jax.ShapeDtypeStruct((64, WAVE), f32),
        ),
        in_specs=[hbm, hbm],
        out_specs=(hbm, hbm, hbm),
        scratch_shapes=[
            pltpu.VMEM((64, 2 * WAVE), f32),
            pltpu.VMEM((OWN, WAVE), bf16),
            dma((11,)),
        ],
        compiler_params=pltpu.CompilerParams(vmem_limit_bytes=63 << 20),
        name="finish",
    )(filtered, sums)


def solution(mesh):
    placed = (P("dom", "band"), P("dom", None, None), P("dom", None), P("dom"))
    return jax.shard_map(
        shards,
        mesh=mesh,
        in_specs=placed,
        out_specs=(P("dom", "band"), P("dom", "band"), P("dom", "band")),
        check_vma=False,
    )
```
